512 devices in a mesh: blk: 64 (over x, z_hi, y), width: 8 (over z_lo, core).
Axes of the slice: x: 4, y: 8, z: 8 (z_hi: 2, z_lo: 4; z = z_hi * 4 + z_lo), core: 2. Of those that a mesh axis runs over, the one named last changes fastest.
Arguments:
- tokens: bfloat16 [352, 8192], P(None, ('width', 'blk')), may hold values from -6 to 6
- gate_weight: bfloat16 [8192, 16384], P('width', 'blk'), may hold values from -0.0625 to 0.0625
- up_weight: bfloat16 [8192, 16384], P('width', 'blk'), may hold values from -0.0625 to 0.0625
- down_weight: bfloat16 [16384, 8192], P('blk', 'width'), may hold values from -0.046875 to 0.046875
- cotangent: bfloat16 [352, 8192], P(None, ('width', 'blk')), may hold values from -6 to 6
Outputs:
- output: bfloat16 [352, 8192], P(None, ('width', 'blk'))
- input_grad: bfloat16 [352, 8192], P(None, ('width', 'blk'))
- gate_weight_grad: float32 [8192, 16384], P('width', 'blk')
- up_weight_grad: float32 [8192, 16384], P('width', 'blk')
- down_weight_grad: float32 [16384, 8192], P('blk', 'width')
The draws below stay inside these ranges and needn't reach their ends.
All inputs are finite; a program needn't handle non-finite values.
Results may differ from the reference program's by a relative error of at most 0.022.
Values may be sent and summed in bfloat16 or wider, within the bound.
A program may use at most 64 MiB of HBM per device.

```python
import jax
import jax.numpy as jnp

D = 8192
FF = 16384
TOKENS = 352


def levels(key, dims, shards, smallest, largest):
    loudness = 1.0
    for position, blocks in shards:
        heights = jax.random.uniform(jax.random.fold_in(jax.random.fold_in(key, 6), position), (blocks,), jnp.float32, smallest / len(shards), largest / len(shards))
        loudness = loudness * jnp.repeat(jnp.exp(heights), dims[position] // blocks).reshape((-1,) + (1,) * (len(dims) - 1 - position))
    return loudness


def bell_draw(rng, extent, width, reach, pieces=(), kind=jnp.bfloat16):
    drawn = width * jax.random.normal(rng, extent, jnp.float32)
    if pieces:
        drawn = drawn * levels(rng, extent, pieces, -0.22, 0.18)
    return jnp.clip(drawn, -reach, reach).astype(kind)


def setup_inputs(seed: int = 0) -> dict:
    keys = jax.random.split(jax.random.key(seed), 6)
    return {
        "tokens": bell_draw(keys[0], (TOKENS, D), 1.0, 6.0, ((1, 512),)),
        "gate_weight": bell_draw(keys[1], (D, FF), D ** -0.5, 0.0625, ((0, 8), (1, 64))),
        "up_weight": bell_draw(keys[2], (D, FF), D ** -0.5, 0.0625, ((0, 8), (1, 64))),
        "down_weight": bell_draw(keys[3], (FF, D), FF ** -0.5, 0.046875, ((0, 64), (1, 8))),
        "cotangent": bell_draw(keys[4], (TOKENS, D), 1.0, 6.0, ((1, 512),)),
    }


def reference(tokens, gate_weight, up_weight, down_weight, cotangent):
    gate_pre = jnp.dot(tokens, gate_weight, preferred_element_type=jnp.float32)
    up_pre = jnp.dot(tokens, up_weight, preferred_element_type=jnp.float32)
    sigmoid_gate = jax.nn.sigmoid(gate_pre)
    hidden = (gate_pre * sigmoid_gate * up_pre).astype(jnp.bfloat16)
    output = jnp.dot(hidden, down_weight, preferred_element_type=jnp.float32).astype(jnp.bfloat16)
    down_weight_grad = jnp.dot(hidden.T, cotangent, preferred_element_type=jnp.float32)
    hidden_grad = jnp.dot(cotangent, down_weight.T, preferred_element_type=jnp.float32)
    gate_grad = (hidden_grad * up_pre * sigmoid_gate * (1.0 + gate_pre * (1.0 - sigmoid_gate))).astype(jnp.bfloat16)
    up_grad = (hidden_grad * gate_pre * sigmoid_gate).astype(jnp.bfloat16)
    gate_weight_grad = jnp.dot(tokens.T, gate_grad, preferred_element_type=jnp.float32)
    up_weight_grad = jnp.dot(tokens.T, up_grad, preferred_element_type=jnp.float32)
    input_grad = jnp.dot(gate_grad, gate_weight.T, preferred_element_type=jnp.float32)
    input_grad = input_grad + jnp.dot(up_grad, up_weight.T, preferred_element_type=jnp.float32)
    return (output, input_grad.astype(jnp.bfloat16), gate_weight_grad, up_weight_grad, down_weight_grad)
```

```python
import functools

import jax
import jax.numpy as jnp
from jax import lax
from jax.experimental import pallas as pl
from jax.experimental.pallas import tpu as pltpu
from jax.sharding import PartitionSpec as P

MESH = pl.DeviceIdType.MESH
X, ZH, Y = 4, 2, 8
ZL, CORES = 4, 2
F32, BF16 = jnp.float32, jnp.bfloat16


def mm(left, right, dims):
    return lax.dot_general(left, right, ((dims[:1], dims[1:]), ((), ())), preferred_element_type=F32)


class Sems:
    def __init__(self, send, recv):
        self.send, self.recv, self.used, self.live = send, recv, 0, []

    def copy(self, src, dst, device):
        i = self.used
        self.used += 1
        c = pltpu.make_async_remote_copy(
            src_ref=src, dst_ref=dst, send_sem=self.send.at[i], recv_sem=self.recv.at[i],
            device_id=device, device_id_type=MESH,
        )
        c.start()
        self.live.append(c)
        return c


def turns(*gens):
    gens = list(gens)
    while gens:
        for g in list(gens):
            try:
                next(g)
            except StopIteration:
                gens.remove(g)


def kernel(
    tok_ref, cot_ref, gw_hbm, uw_hbm, dw_hbm,
    out_ref, inp_ref, gwg_hbm, uwg_hbm, dwg_hbm,
    gw, uw, dw, gwg, uwg, dwg, G, PF, P16, C1, SZ, RZ, H, OT, SA, RA, SX, RX, ACC, SF, RF, SD, RD, SY, RY, SW, RW,
    send_sem, recv_sem, local_sem,
):
    b, w = lax.axis_index("blk"), lax.axis_index("width")
    x, zh, y = b // (ZH * Y), (b // Y) % ZH, b % Y
    zl, core = w // CORES, w % CORES
    oz, oc = 1 - zh, 1 - core
    tokens = tok_ref.shape[0]
    T = G.shape[-1]

    def xs(d):
        return (x + d) % X

    def ys(d):
        return (y + d) % Y

    def at_xy(d_x, d_y):
        return ((xs(d_x) * ZH + zh) * Y + ys(d_y), w)

    xdev = {d: at_xy(d, 0) for d in range(1, X)}
    ydev = {1: at_xy(0, 1), -1: at_xy(0, Y - 1)}
    xdev[-1] = xdev[X - 1]
    zdev = ((x * ZH + oz) * Y + y, w)
    cdev = (b, zl * CORES + oc)
    ldev = {d: (b, ((zl + d) % ZL) * CORES + core) for d in range(1, ZL)}

    loads = [
        pltpu.make_async_copy(s, d, local_sem.at[i])
        for i, (s, d) in enumerate(((gw_hbm, gw), (uw_hbm, uw), (dw_hbm, dw)))
    ]
    for c in loads:
        c.start()

    barrier = pltpu.get_barrier_semaphore()
    partners = [xdev[d] for d in range(1, X)] + [ydev[1], ydev[-1], zdev, cdev] + [ldev[d] for d in range(1, ZL)]
    for p in partners:
        pl.semaphore_signal(barrier, inc=1, device_id=p, device_id_type=MESH)

    eye = (
        lax.broadcasted_iota(jnp.int32, (16, 16), 0) == lax.broadcasted_iota(jnp.int32, (16, 16), 1)
    ).astype(F32).astype(BF16)
    for t, ref in enumerate((tok_ref, cot_ref)):
        G[t, x, zh, y] = mm(eye, jnp.pad(ref[...], ((0, T - tokens), (0, 0))), (1, 1)).astype(BF16)
    pl.semaphore_wait(barrier, len(partners))

    sems = Sems(send_sem, recv_sem)

    def gather_a(t):
        own = G.at[t, x, zh, y]
        xm = {d: sems.copy(own, own, xdev[d]) for d in range(1, X)}
        yield
        R, L = {}, {}
        far = {d: (4, 3) if d % 2 == 0 else (3, 4) for d in range(X)}
        for k in range(5):
            for d in range(X):
                if k == 0 and d > 0:
                    xm[d].wait_recv()
                for M, sign, n in ((R, 1, far[d][0]), (L, -1, far[d][1])):
                    if 0 < k <= n:
                        M[k - 1, d].wait_recv()
                    if k < n:
                        piece = G.at[t, xs(X - d), zh, ys(Y - sign * k)]
                        M[k, d] = sems.copy(piece, piece, ydev[sign])
                yield

    def gather_b(t, zm):
        zm.wait_recv()
        R, L, XR, XL, XF = {}, {}, {}, {}, {}
        done = []

        def spread(k):
            yk = ys(Y - k)
            piece = G.at[t, x, oz, yk]
            XR[k] = sems.copy(piece, piece, xdev[1])
            XL[k] = sems.copy(piece, piece, xdev[-1])
            done.append(k)

        def forward(k):
            yk = ys(Y - k)
            if k % 2 == 0:
                XR[k].wait_recv()
                piece = G.at[t, xs(X - 1), oz, yk]
                XF[k] = sems.copy(piece, piece, xdev[1])
            else:
                XL[k].wait_recv()
                piece = G.at[t, xs(1), oz, yk]
                XF[k] = sems.copy(piece, piece, xdev[-1])

        for k in range(5):
            for M, sign, n in ((R, 1, 4), (L, -1, 3)):
                if 0 < k <= n:
                    M[k - 1].wait_recv()
                if k < n:
                    piece = G.at[t, x, oz, ys(Y - sign * k)]
                    M[k] = sems.copy(piece, piece, ydev[sign])
            old = list(done)
            for sign, n in ((1, 4), (-1, 3)):
                if k <= n and (k > 0 or sign > 0):
                    spread(sign * k)
            yield
            for j in old:
                if j not in XF:
                    forward(j)
            yield
        for j in done:
            if j not in XF:
                forward(j)
        yield
        for j in done:
            (XL if j % 2 == 0 else XR)[j].wait_recv()
            XF[j].wait_recv()

    def width_sum(a0, na, result):
        a = pl.ds(a0, na)
        P16[a] = PF[a, oc].astype(BF16)
        cm = sems.copy(P16.at[a], C1.at[a], cdev)
        yield
        cm.wait_recv()
        zm = {}
        for d in (2, 1, 3):
            j = (zl + d) % ZL
            SZ[d, a] = (PF[a, core, j] + C1[a, j].astype(F32)).astype(BF16)
            zm[d] = sems.copy(SZ.at[d, a], RZ.at[d, a], ldev[d])
        total = PF[a, core, zl] + C1[a, zl].astype(F32)
        yield
        for d in (1, 3, 2):
            zm[d].wait_recv()
            total = total + RZ[d, a].astype(F32)
        PF[a, core, zl] = total
        result()

    def width_gather(a0, na):
        a = pl.ds(a0, na)
        own = H.at[a, core, zl]
        zm = {d: sems.copy(own, own, ldev[d]) for d in (2, 1, 3)}
        cm = {0: sems.copy(own, own, cdev)}
        yield
        for d in (1, 3, 2):
            zm[d].wait_recv()
            piece = H.at[a, core, (zl + ZL - d) % ZL]
            cm[d] = sems.copy(piece, piece, cdev)
            yield
        for d in (0, 1, 3, 2):
            cm[d].wait_recv()

    def make_hidden():
        g, u = PF[0, core, zl], PF[1, core, zl]
        s = 1.0 / (1.0 + jnp.exp(-g))
        H[0, core, zl] = (g * s * u).astype(BF16)

    def make_grads():
        g, u, h = PF[0, core, zl], PF[1, core, zl], PF[2, core, zl]
        s = 1.0 / (1.0 + jnp.exp(-g))
        H[1, core, zl] = (h * u * s * (1.0 + g * (1.0 - s))).astype(BF16)
        H[2, core, zl] = (h * g * s).astype(BF16)

    def scatter_a(t):
        R, L, xm = {}, {}, {}
        far = {d: (4, 3) if d % 2 == 0 else (3, 4) for d in range(X)}
        order = (1, 2, 3, 0)
        for k in range(5):
            for d in order:
                for M, i, sign, n in ((R, 0, 1, far[d][0]), (L, 1, -1, far[d][1])):
                    if 0 < k <= n:
                        M[k - 1, d].wait_recv()
                    if k < n:
                        v = OT[t, xs(d), zh, ys(Y + sign * (n - k))]
                        if k > 0:
                            v = v + RA[t, i, k - 1, d].astype(F32)
                        SA[t, i, k, d] = v.astype(BF16)
                        M[k, d] = sems.copy(SA.at[t, i, k, d], RA.at[t, i, k, d], ydev[sign])
                if k == 4:
                    v = OT[t, xs(d), zh, y]
                    v = v + RA[t, 0, far[d][0] - 1, d].astype(F32) + RA[t, 1, far[d][1] - 1, d].astype(F32)
                    if d > 0:
                        SX[t, d] = v.astype(BF16)
                        xm[d] = sems.copy(SX.at[t, d], RX.at[t, d], xdev[d])
                    else:
                        ACC[t] = v
                yield
        for d in order[:-1]:
            xm[d].wait_recv()
            ACC[t] += RX[t, d].astype(F32)

    def scatter_b(t):
        order = (4, 5, 3, 6, 2, 7, 1, 0)
        F, D = {}, {}
        for j in order:
            SF[t, j] = OT[t, xs(2), oz, ys(j)].astype(BF16)
            F[j] = sems.copy(SF.at[t, j], RF.at[t, j], xdev[1 if j % 2 == 0 else -1])
        yield
        for j in order:
            for i, sign in ((0, 1), (1, -1)):
                if (j % 2 == 0) != (sign > 0):
                    SD[t, i, j] = OT[t, xs(sign % X), oz, ys(j)].astype(BF16)
                    D[i, j] = sems.copy(SD.at[t, i, j], RD.at[t, i, j], xdev[sign])
        yield
        for n, j in enumerate(order):
            i, sign = (0, 1) if j % 2 == 0 else (1, -1)
            F[j].wait_recv()
            SD[t, i, j] = (OT[t, xs(sign % X), oz, ys(j)] + RF[t, j].astype(F32)).astype(BF16)
            D[i, j] = sems.copy(SD.at[t, i, j], RD.at[t, i, j], xdev[sign])
            if n % 2:
                yield

        def take(j):
            D[0, j].wait_recv()
            D[1, j].wait_recv()
            return OT[t, x, oz, ys(j)] + RD[t, 0, j].astype(F32) + RD[t, 1, j].astype(F32)

        R, L = {}, {}
        for k in range(4):
            for M, i, sign, n in ((R, 0, 1, 4), (L, 1, -1, 3)):
                if k < n:
                    v = take(sign * (n - k) % Y)
                    if k > 0:
                        M[k - 1].wait_recv()
                        v = v + RY[t, i, k - 1].astype(F32)
                    SY[t, i, k] = v.astype(BF16)
                    M[k] = sems.copy(SY.at[t, i, k], RY.at[t, i, k], ydev[sign])
            yield
        v = take(0)
        L[2].wait_recv()
        v = v + RY[t, 1, 2].astype(F32)
        R[3].wait_recv()
        v = v + RY[t, 0, 3].astype(F32)
        SW[t] = v.astype(BF16)
        wm = sems.copy(SW.at[t], RW.at[t], zdev)
        yield
        wm.wait_recv()

    def finish(t, ref):
        v = (ACC[t] + RW[t].astype(F32)).astype(BF16)
        ref[...] = mm(v, eye, (0, 0))[:tokens].astype(BF16)

    def hid(i):
        return H[i].reshape(dw.shape[0], T)

    def rows(t, i):
        return G[t, i].reshape(ZH * Y * 16, T)

    span = ZH * Y * 16

    def put(t, i, v):
        OT[t, i] = v.reshape(ZH, Y, 16, T)

    def grads(t):
        for i in range(X):
            s = pl.ds(i * span, span)
            if t == 0:
                dwg[:, s] = mm(hid(0), rows(1, i), (1, 1))
                yield
            else:
                gwg[s, :] = mm(rows(0, i), hid(1), (1, 1))
                yield
                uwg[s, :] = mm(rows(0, i), hid(2), (1, 1))
                yield

    zm = [None, None]
    for t in range(2):
        own = G.at[t, x, zh, y]
        zm[t] = sems.copy(own, own, zdev)
    tok = [gather_a(0), gather_b(0, zm[0])]
    turns(*tok)
    cot = [gather_a(1), gather_b(1, zm[1])]
    for g in cot:
        next(g)
    full = (CORES, ZL, -1, T)
    loads[0].wait()
    loads[1].wait()
    PF[0] = mm(gw[...], G[0].reshape(-1, T), (0, 0)).reshape(PF.shape[1:])
    PF[1] = mm(uw[...], G[0].reshape(-1, T), (0, 0)).reshape(PF.shape[1:])

    def early():
        yield from width_sum(0, 2, make_hidden)
        yield from width_gather(0, 1)

    turns(*cot, early())
    loads[2].wait()
    PF[2] = mm(dw[...], G[1].reshape(-1, T), (1, 0)).reshape(PF.shape[1:])
    late = width_sum(2, 1, make_grads)
    next(late)
    for i in range(X):
        put(0, i, mm(dw[:, i * span : (i + 1) * span], hid(0), (0, 0)))

    def mid():
        yield from late
        yield from width_gather(1, 2)

    out = [scatter_a(0), scatter_b(0)]
    turns(mid(), *out, grads(0))
    stores = [pltpu.make_async_copy(dwg, dwg_hbm, local_sem.at[3])]
    stores[0].start()
    for i in range(X):
        s = pl.ds(i * span, span)
        put(1, i, mm(gw[s, :], hid(1), (1, 0)) + mm(uw[s, :], hid(2), (1, 0)))
    turns(scatter_a(1), scatter_b(1), grads(1))
    stores.append(pltpu.make_async_copy(gwg, gwg_hbm, local_sem.at[4]))
    stores.append(pltpu.make_async_copy(uwg, uwg_hbm, local_sem.at[5]))
    stores[1].start()
    stores[2].start()
    finish(0, out_ref)
    finish(1, inp_ref)
    for c in sems.live:
        c.wait_send()
    for c in stores:
        c.wait()
    assert sems.used <= send_sem.shape[0], sems.used


def body(tokens, gate_weight, up_weight, down_weight, cotangent):
    n, (depth, hidden) = tokens.shape[0], gate_weight.shape
    T = -(-n // 128) * 128
    V = pltpu.VMEM
    part = hidden // (CORES * ZL)
    scratch = [
        V(gate_weight.shape, BF16), V(up_weight.shape, BF16), V(down_weight.shape, BF16),
        V(gate_weight.shape, F32), V(up_weight.shape, F32), V(down_weight.shape, F32),
        V((2, X, ZH, Y, 16, T), BF16),
        V((3, CORES, ZL, part, T), F32),
        V((3, ZL, part, T), BF16), V((3, ZL, part, T), BF16),
        V((ZL, 3, part, T), BF16), V((ZL, 3, part, T), BF16),
        V((3, CORES, ZL, part, T), BF16),
        V((2, X, ZH, Y, 16, T), F32),
        V((2, 2, 4, X, 16, T), BF16), V((2, 2, 4, X, 16, T), BF16),
        V((2, X, 16, T), BF16), V((2, X, 16, T), BF16),
        V((2, 16, T), F32),
        V((2, Y, 16, T), BF16), V((2, Y, 16, T), BF16),
        V((2, 2, Y, 16, T), BF16), V((2, 2, Y, 16, T), BF16),
        V((2, 2, 4, 16, T), BF16), V((2, 2, 4, 16, T), BF16),
        V((2, 16, T), BF16), V((2, 16, T), BF16),
        pltpu.SemaphoreType.DMA((300,)),
        pltpu.SemaphoreType.DMA((300,)),
        pltpu.SemaphoreType.DMA((6,)),
    ]
    vm, anywhere = pl.BlockSpec(memory_space=V), pl.BlockSpec(memory_space=pl.ANY)
    S = jax.ShapeDtypeStruct
    return pl.pallas_call(
        kernel,
        out_shape=(
            S(tokens.shape, BF16), S(tokens.shape, BF16),
            S(gate_weight.shape, F32), S(up_weight.shape, F32), S(down_weight.shape, F32),
        ),
        in_specs=[vm, vm, anywhere, anywhere, anywhere],
        out_specs=(vm, vm, anywhere, anywhere, anywhere),
        scratch_shapes=scratch,
        compiler_params=pltpu.CompilerParams(
            collective_id=0, has_side_effects=True, vmem_limit_bytes=48 * 2**20
        ),
        cost_estimate=pl.CostEstimate(flops=18 * n * depth * hidden, bytes_accessed=18 * depth * hidden, transcendentals=0),
        name="ffn",
    )(tokens, cotangent, gate_weight, up_weight, down_weight)


def solution(mesh):
    return jax.shard_map(
        body,
        mesh=mesh,
        in_specs=(
            P(None, ("width", "blk")),
            P("width", "blk"),
            P("width", "blk"),
            P("blk", "width"),
            P(None, ("width", "blk")),
        ),
        out_specs=(
            P(None, ("width", "blk")),
            P(None, ("width", "blk")),
            P("width", "blk"),
            P("width", "blk"),
            P("blk", "width"),
        ),
        check_vma=False,
    )
```

```python
import functools

import jax
import jax.numpy as jnp
from jax import lax
from jax.experimental import pallas as pl
from jax.experimental.pallas import tpu as pltpu
from jax.sharding import PartitionSpec as P

MESH = pl.DeviceIdType.MESH
X, ZH, Y = 4, 2, 8
ZL, CORES = 4, 2
F32, BF16 = jnp.float32, jnp.bfloat16


def mm(left, right, dims):
    return lax.dot_general(left, right, ((dims[:1], dims[1:]), ((), ())), preferred_element_type=F32)


class Sems:
    def __init__(self, send, recv):
        self.send, self.recv, self.used, self.live = send, recv, 0, []

    def copy(self, src, dst, device):
        i = self.used
        self.used += 1
        c = pltpu.make_async_remote_copy(
            src_ref=src, dst_ref=dst, send_sem=self.send.at[i], recv_sem=self.recv.at[i],
            device_id=device, device_id_type=MESH,
        )
        c.start()
        self.live.append(c)
        return c


def turns(*gens):
    gens = list(gens)
    while gens:
        for g in list(gens):
            try:
                next(g)
            except StopIteration:
                gens.remove(g)


def kernel(
    tok_hbm, cot_hbm, gw_hbm, uw_hbm, dw_hbm,
    out_hbm, inp_hbm, gwg_hbm, uwg_hbm, dwg_hbm,
    io, gw, uw, dw, gwT, uwT, dwT, gwg, uwg, dwg, G, PF, P16, C1, SZ, RZ, H, OT,
    SA, RA, SF, RF, SX, RX, ACC, SD, RD, SY, RY, SW, RW,
    send_sem, recv_sem, local_sem,
):
    b, w = lax.axis_index("blk"), lax.axis_index("width")
    x, zh, y = b // (ZH * Y), (b // Y) % ZH, b % Y
    zl, core = w // CORES, w % CORES
    oz, oc = 1 - zh, 1 - core
    tokens = io.shape[-1]
    T = G.shape[-1]
    span = ZH * Y * 16

    def xs(d):
        return (x + d % X) % X

    def ys(d):
        return (y + d % Y) % Y

    xdev = {d: ((xs(d) * ZH + zh) * Y + y, w) for d in range(1, X)}
    ydev = {d: ((x * ZH + zh) * Y + ys(d), w) for d in (1, -1, 2, -2, 3, -3, 4)}
    zdev = ((x * ZH + oz) * Y + y, w)
    cdev = (b, zl * CORES + oc)
    ldev = {d: (b, ((zl + d) % ZL) * CORES + core) for d in range(1, ZL)}

    barrier = pltpu.get_barrier_semaphore()
    partners = [zdev] + list(ldev.values()) + list(ydev.values()) + list(xdev.values()) + [cdev]
    for p in partners:
        pl.semaphore_signal(barrier, inc=1, device_id=p, device_id_type=MESH)

    loads = [
        pltpu.make_async_copy(s, d, local_sem.at[i])
        for i, (s, d) in enumerate(
            ((tok_hbm, io.at[0]), (cot_hbm, io.at[1]), (gw_hbm, gw), (uw_hbm, uw), (dw_hbm, dw))
        )
    ]
    for c in loads:
        c.start()
    for t in range(2):
        loads[t].wait()
        G[t, 0, zh, y] = jnp.pad(io[t].astype(F32), ((0, 0), (0, T - tokens))).astype(BF16)
    for c in loads[2:]:
        c.wait()
    for i in range(X):
        s = slice(i * span, (i + 1) * span)
        gwT[i] = gw[s, :].T
        uwT[i] = uw[s, :].T
        dwT[i] = dw[:, s].T
    pl.semaphore_wait(barrier, len(partners))

    sems = Sems(send_sem, recv_sem)

    def cols(i):
        return pl.ds(pl.multiple_of(i * span, span), span)

    def block(t, d):
        return G[t, d].reshape(span, T)

    def part(t, d):
        i = xs(-d)
        v = block(t, d)
        if t == 0:
            new = (mm(gwT[i], v, (1, 0)), mm(uwT[i], v, (1, 0)))
        else:
            new = (mm(dw[:, cols(i)], v, (1, 0)),)
        for n, p in enumerate(new):
            p = p.reshape(PF.shape[1:])
            PF[2 * t + n] = p if d == 0 else PF[2 * t + n] + p

    def gather(t, zm):
        own, rest = G.at[t, 0, zh, y], G.at[t, pl.ds(1, X - 1), zh, y]
        near = (1, -1, 2, -2)
        xm = {d: sems.copy(own, G.at[t, d, zh, y], xdev[d]) for d in (2, 1, 3)}
        N1 = {e: sems.copy(own, own, ydev[e]) for e in near}
        yield
        for d in (1, 3, 2):
            xm[d].wait_recv()
        N2 = {e: sems.copy(rest, rest, ydev[e]) for e in (2, -2, 1, -1)}
        yield
        if t == 0:
            zm.wait_recv()
        other = G.at[t, 0, oz, y]
        B = {e: sems.copy(other, other, ydev[e]) for e in (1, -1, 2, -2, 3, -3, 4)}
        XB = {}

        def spread(e):
            piece = G.at[t, 0, oz, ys(-e)]
            for d in (2, 1, 3):
                XB[e, d] = sems.copy(piece, G.at[t, d, oz, ys(-e)], xdev[d])

        spread(0)
        yield
        F = []
        for s, half in ((1, pl.ds(0, X // 2)), (-1, pl.ds(X // 2, X // 2))):
            N1[2 * s].wait_recv()
            N2[2 * s].wait_recv()
            piece = G.at[t, half, zh, ys(-2 * s)]
            F.append(sems.copy(piece, piece, ydev[2 * s]))
            piece = G.at[t, :, zh, ys(-2 * s)]
            F.append(sems.copy(piece, piece, ydev[s]))
        yield
        for e in (1, -1, 2, -2, 3, -3, 4):
            B[e].wait_recv()
            spread(e)
            if e != 1 and e != 2 and e != 3:
                yield
        for e in (1, -1):
            N1[e].wait_recv()
            N2[e].wait_recv()
        for c in F:
            c.wait_recv()
        part(t, 0)
        yield
        for d in (1, 3, 2):
            for e in (0, 1, -1, 2, -2, 3, -3, 4):
                XB[e, d].wait_recv()
            part(t, d)

    def width_sum(a0, na, result):
        a = pl.ds(a0, na)
        P16[a] = PF[a, oc].astype(BF16)
        cm = sems.copy(P16.at[a], C1.at[a], cdev)
        yield
        cm.wait_recv()
        zm = {}
        for d in (3, 2, 1):
            j = (zl + d) % ZL
            SZ[d, a] = (PF[a, core, j] + C1[a, j].astype(F32)).astype(BF16)
            zm[d] = sems.copy(SZ.at[d, a], RZ.at[d, a], ldev[d])
        total = PF[a, core, zl] + C1[a, zl].astype(F32)
        PF[a, core, zl] = total
        yield
        for d in (1, 3, 2):
            zm[d].wait_recv()
            total = total + RZ[d, a].astype(F32)
        PF[a, core, zl] = total
        result()

    def width_gather(a0, na):
        a = pl.ds(a0, na)
        own = H.at[a, core, zl]
        zm = {d: sems.copy(own, own, ldev[d]) for d in (3, 2, 1)}
        cm = {0: sems.copy(own, own, cdev)}
        yield
        for d in (1, 3, 2):
            zm[d].wait_recv()
            piece = H.at[a, core, (zl + ZL - d) % ZL]
            cm[d] = sems.copy(piece, piece, cdev)
        yield
        for d in (0, 1, 3, 2):
            cm[d].wait_recv()

    def make_hidden():
        g, u = PF[0, core, zl], PF[1, core, zl]
        s = 1.0 / (1.0 + jnp.exp(-g))
        H[0, core, zl] = (g * s * u).astype(BF16)

    def make_grads():
        g, u, h = PF[0, core, zl], PF[1, core, zl], PF[2, core, zl]
        s = 1.0 / (1.0 + jnp.exp(-g))
        H[1, core, zl] = (h * u * s * (1.0 + g * (1.0 - s))).astype(BF16)
        H[2, core, zl] = (h * g * s).astype(BF16)

    def scatter_a(t):
        halves = {1: pl.ds(0, X // 2), -1: pl.ds(X // 2, X // 2)}
        F4, M = {}, {}

        def send(i, v, device):
            SA[t, i] = v.astype(BF16)
            M[i] = sems.copy(SA.at[t, i], RA.at[t, i], device)

        for i, s in enumerate((1, -1)):
            SF[t, i] = OT[t, halves[s], zh, ys(4)].astype(BF16)
            F4[i] = sems.copy(SF.at[t, i], RF.at[t, i], ydev[2 * s])
            send(i, OT[t, :, zh, ys(3 * s)], ydev[s])
        yield
        for i, s in enumerate((1, -1)):
            send(2 + i, OT[t, :, zh, ys(s)], ydev[s])
        yield
        for i, s in enumerate((1, -1)):
            M[i].wait_recv()
            F4[i].wait_recv()
            OT[t, halves[s], zh, ys(2 * s)] += RF[t, i].astype(F32)
            send(4 + i, OT[t, :, zh, ys(2 * s)] + RA[t, i].astype(F32), ydev[2 * s])
        yield
        v = OT[t, :, zh, y]
        for i in (2, 3, 4, 5):
            M[i].wait_recv()
            v = v + RA[t, i].astype(F32)
        SX[t] = v[1:].astype(BF16)
        xm = {d: sems.copy(SX.at[t, d - 1], RX.at[t, d - 1], xdev[d]) for d in (2, 1, 3)}
        ACC[t] = v[0]
        yield
        for d in (1, 3, 2):
            xm[d].wait_recv()
            ACC[t] += RX[t, d - 1].astype(F32)

    def scatter_b(t):
        order = (4, -3, 3, -2, 2, -1, 1, 0)
        groups = ((0, 3), (3, 5), (5, 8))
        D, M = {}, {}
        for lo, hi in groups:
            for n in range(lo, hi):
                SD[t, :, n] = OT[t, pl.ds(1, X - 1), oz, ys(order[n])].astype(BF16)
            for d in (2, 1, 3):
                at = (t, d - 1, pl.ds(lo, hi - lo))
                D[lo, d] = sems.copy(SD.at[at], RD.at[at], xdev[d])
        yield
        for lo, hi in groups:
            for d in (1, 3, 2):
                D[lo, d].wait_recv()
            for n in range(lo, hi):
                v = OT[t, 0, oz, ys(order[n])]
                for d in range(1, X):
                    v = v + RD[t, d - 1, n].astype(F32)
                if order[n]:
                    SY[t, n] = v.astype(BF16)
                    M[n] = sems.copy(SY.at[t, n], RY.at[t, n], ydev[order[n]])
            yield
        for n in (5, 6, 3, 4, 1, 2, 0):
            M[n].wait_recv()
            v = v + RY[t, n].astype(F32)
        SW[t] = v.astype(BF16)
        M[7] = sems.copy(SW.at[t], RW.at[t], zdev)
        yield
        M[7].wait_recv()

    def hid(i):
        return H[i].reshape(dw.shape[0], T)

    def grads():
        for d in range(X):
            i = xs(-d)
            dwg[:, cols(i)] = mm(hid(0), block(1, d), (1, 1))
            yield
            gwg[cols(i), :] = mm(block(0, d), hid(1), (1, 1))
            yield
            uwg[cols(i), :] = mm(block(0, d), hid(2), (1, 1))
            yield

    def put(t, d, v):
        OT[t, d] = v.reshape(ZH, Y, 16, T)

    def drain(g):
        for _ in g:
            pass

    both = G.at[:, 0, zh, y]
    zm = sems.copy(both, both, zdev)
    tok, cot = gather(0, zm), gather(1, zm)
    left = True
    while left:
        left = False
        for _ in tok:
            left = True
            break
        if left:
            next(cot)
    pre = width_sum(0, 2, make_hidden)
    next(pre)
    next(pre)
    drain(cot)
    post = width_sum(2, 1, make_grads)
    next(post)
    next(post)
    drain(pre)
    fore = width_gather(0, 1)
    next(fore)
    drain(post)
    back = width_gather(1, 2)
    next(back)
    drain(fore)
    for d in range(X):
        put(0, d, mm(dwT[xs(d)], hid(0), (1, 0)))
    out = [scatter_b(0), scatter_a(0)]
    for g in out:
        next(g)
    drain(back)
    for d in range(X):
        i = xs(d)
        put(1, d, mm(gw[cols(i), :], hid(1), (1, 0)) + mm(uw[cols(i), :], hid(2), (1, 0)))
    turns(scatter_b(1), scatter_a(1), *out, grads())
    stores = []

    def store(src, dst):
        c = pltpu.make_async_copy(src, dst, local_sem.at[5 + len(stores)])
        c.start()
        stores.append(c)

    for src, dst in ((dwg, dwg_hbm), (gwg, gwg_hbm), (uwg, uwg_hbm)):
        store(src, dst)
    for t, ref in enumerate((out_hbm, inp_hbm)):
        io[t] = (ACC[t] + RW[t].astype(F32)).astype(BF16)[:, :tokens]
        store(io.at[t], ref)
    for c in sems.live:
        c.wait_send()
    for c in stores:
        c.wait()
    assert sems.used <= send_sem.shape[0], sems.used


def hand_on(*refs):
    n = len(refs) // 2
    copies = [pltpu.make_async_copy(refs[i], refs[n + i], refs[-1].at[i]) for i in range(n)]
    for c in copies:
        c.start()
    for c in copies:
        c.wait()


def body(tokens, gate_weight, up_weight, down_weight, cotangent):
    n, (depth, hidden) = tokens.shape[0], gate_weight.shape
    T = -(-n // 128) * 128
    V = pltpu.VMEM
    part, span = hidden // (CORES * ZL), ZH * Y * 16
    scratch = [
        V((2, 16, n), BF16),
        V(gate_weight.shape, BF16), V(up_weight.shape, BF16), V(down_weight.shape, BF16),
        V((X, hidden, span), BF16), V((X, hidden, span), BF16), V((X, span, hidden), BF16),
        V(gate_weight.shape, F32), V(up_weight.shape, F32), V(down_weight.shape, F32),
        V((2, X, ZH, Y, 16, T), BF16),
        V((3, CORES, ZL, part, T), F32),
        V((3, ZL, part, T), BF16), V((3, ZL, part, T), BF16),
        V((ZL, 3, part, T), BF16), V((ZL, 3, part, T), BF16),
        V((3, CORES, ZL, part, T), BF16),
        V((2, X, ZH, Y, 16, T), F32),
        V((2, 6, X, 16, T), BF16), V((2, 6, X, 16, T), BF16),
        V((2, 2, X // 2, 16, T), BF16), V((2, 2, X // 2, 16, T), BF16),
        V((2, X - 1, 16, T), BF16), V((2, X - 1, 16, T), BF16),
        V((2, 16, T), F32),
        V((2, X - 1, Y, 16, T), BF16), V((2, X - 1, Y, 16, T), BF16),
        V((2, Y, 16, T), BF16), V((2, Y, 16, T), BF16),
        V((2, 16, T), BF16), V((2, 16, T), BF16),
        pltpu.SemaphoreType.DMA((200,)),
        pltpu.SemaphoreType.DMA((200,)),
        pltpu.SemaphoreType.DMA((10,)),
    ]
    anywhere = pl.BlockSpec(memory_space=pl.ANY)
    S = jax.ShapeDtypeStruct
    shapes = (
        S((16, n), BF16), S((16, n), BF16),
        S(gate_weight.shape, F32), S(up_weight.shape, F32), S(down_weight.shape, F32),
    )
    outs = pl.pallas_call(
        kernel,
        out_shape=shapes,
        in_specs=[anywhere] * 5,
        out_specs=(anywhere,) * 5,
        scratch_shapes=scratch,
        compiler_params=pltpu.CompilerParams(
            collective_id=0, has_side_effects=True, vmem_limit_bytes=60 * 2**20
        ),
        cost_estimate=pl.CostEstimate(flops=18 * n * depth * hidden, bytes_accessed=18 * depth * hidden, transcendentals=0),
        name="ffn",
    )(tokens.T, cotangent.T, gate_weight, up_weight, down_weight)
    output, input_grad, *grads = pl.pallas_call(
        hand_on,
        out_shape=shapes,
        in_specs=[anywhere] * 5,
        out_specs=(anywhere,) * 5,
        scratch_shapes=[pltpu.SemaphoreType.DMA((5,))],
        name="hand_on",
    )(*outs)
    return (output.T, input_grad.T, *grads)


def solution(mesh):
    return jax.shard_map(
        body,
        mesh=mesh,
        in_specs=(
            P(None, ("width", "blk")),
            P("width", "blk"),
            P("width", "blk"),
            P("blk", "width"),
            P(None, ("width", "blk")),
        ),
        out_specs=(
            P(None, ("width", "blk")),
            P(None, ("width", "blk")),
            P("width", "blk"),
            P("width", "blk"),
            P("blk", "width"),
        ),
        check_vma=False,
    )
```

```python
import functools

import jax
import jax.numpy as jnp
from jax import lax
from jax.experimental import pallas as pl
from jax.experimental.pallas import tpu as pltpu
from jax.sharding import PartitionSpec as P

MESH = pl.DeviceIdType.MESH
X, ZH, Y = 4, 2, 8
ZL, CORES = 4, 2
F32, BF16 = jnp.float32, jnp.bfloat16


def mm(left, right, dims):
    return lax.dot_general(left, right, ((dims[:1], dims[1:]), ((), ())), preferred_element_type=F32)


class Sems:
    def __init__(self, send, recv):
        self.send, self.recv, self.used, self.live = send, recv, 0, []

    def copy(self, src, dst, device):
        i = self.used
        self.used += 1
        c = pltpu.make_async_remote_copy(
            src_ref=src, dst_ref=dst, send_sem=self.send.at[i], recv_sem=self.recv.at[i],
            device_id=device, device_id_type=MESH,
        )
        c.start()
        self.live.append(c)
        return c


def turns(*gens):
    gens = list(gens)
    while gens:
        for g in list(gens):
            try:
                next(g)
            except StopIteration:
                gens.remove(g)


def kernel(
    tok_hbm, cot_hbm, gw_hbm, uw_hbm, dw_hbm,
    out_hbm, inp_hbm, gwg_hbm, uwg_hbm, dwg_hbm,
    io, gw, uw, dw, gwT, uwT, dwT, gwg, uwg, dwg, G, PF, P16, C1, SZ, RZ, H, OT,
    SA, RA, SF, RF, SX, RX, ACC, SD, RD, SY, RY, SW, RW,
    send_sem, recv_sem, local_sem,
):
    b, w = lax.axis_index("blk"), lax.axis_index("width")
    x, zh, y = b // (ZH * Y), (b // Y) % ZH, b % Y
    zl, core = w // CORES, w % CORES
    oz, oc = 1 - zh, 1 - core
    tokens = io.shape[-1]
    T = G.shape[-1]
    span = ZH * Y * 16

    def xs(d):
        return (x + d % X) % X

    def ys(d):
        return (y + d % Y) % Y

    xdev = {d: ((xs(d) * ZH + zh) * Y + y, w) for d in range(1, X)}
    ydev = {d: ((x * ZH + zh) * Y + ys(d), w) for d in (1, -1, 2, -2, 3, -3, 4)}
    zdev = ((x * ZH + oz) * Y + y, w)
    cdev = (b, zl * CORES + oc)
    ldev = {d: (b, ((zl + d) % ZL) * CORES + core) for d in range(1, ZL)}

    barrier = pltpu.get_barrier_semaphore()
    partners = [zdev] + list(ldev.values()) + list(ydev.values()) + list(xdev.values()) + [cdev]
    for p in partners:
        pl.semaphore_signal(barrier, inc=1, device_id=p, device_id_type=MESH)

    loads = [
        pltpu.make_async_copy(s, d, local_sem.at[i])
        for i, (s, d) in enumerate(
            ((tok_hbm, io.at[0]), (cot_hbm, io.at[1]), (gw_hbm, gw), (uw_hbm, uw), (dw_hbm, dw))
        )
    ]
    for c in loads:
        c.start()
    for t in range(2):
        loads[t].wait()
        G[t, 0, zh, y] = jnp.pad(io[t].astype(F32), ((0, 0), (0, T - tokens))).astype(BF16)
    for c in loads[2:]:
        c.wait()
    for i in range(X):
        s = slice(i * span, (i + 1) * span)
        gwT[i] = gw[s, :].T
        uwT[i] = uw[s, :].T
        dwT[i] = dw[:, s].T
    pl.semaphore_wait(barrier, len(partners))

    sems = Sems(send_sem, recv_sem)

    def cols(i):
        return pl.ds(pl.multiple_of(i * span, span), span)

    def block(t, d):
        return G[t, d].reshape(span, T)

    def part(t, d):
        i = xs(-d)
        v = block(t, d)
        if t == 0:
            new = (mm(gwT[i], v, (1, 0)), mm(uwT[i], v, (1, 0)))
        else:
            new = (mm(dw[:, cols(i)], v, (1, 0)),)
        for n, p in enumerate(new):
            p = p.reshape(PF.shape[1:])
            PF[2 * t + n] = p if d == 0 else PF[2 * t + n] + p

    def gather(t, zm):
        own, rest = G.at[t, 0, zh, y], G.at[t, pl.ds(1, X - 1), zh, y]
        near = (1, -1, 2, -2)
        xm = {d: sems.copy(own, G.at[t, d, zh, y], xdev[d]) for d in (2, 1, 3)}
        N1 = {e: sems.copy(own, own, ydev[e]) for e in near}
        yield
        for d in (1, 3, 2):
            xm[d].wait_recv()
        N2 = {e: sems.copy(rest, rest, ydev[e]) for e in (2, -2, 1, -1)}
        yield
        if t == 0:
            zm.wait_recv()
        other = G.at[t, 0, oz, y]
        B = {e: sems.copy(other, other, ydev[e]) for e in (1, -1, 2, -2, 3, -3, 4)}
        XB = {}

        def spread(e):
            piece = G.at[t, 0, oz, ys(-e)]
            for d in (2, 1, 3):
                XB[e, d] = sems.copy(piece, G.at[t, d, oz, ys(-e)], xdev[d])

        spread(0)
        yield
        F = []
        for s, half in ((1, pl.ds(0, X // 2)), (-1, pl.ds(X // 2, X // 2))):
            N1[2 * s].wait_recv()
            N2[2 * s].wait_recv()
            piece = G.at[t, half, zh, ys(-2 * s)]
            F.append(sems.copy(piece, piece, ydev[2 * s]))
            piece = G.at[t, :, zh, ys(-2 * s)]
            F.append(sems.copy(piece, piece, ydev[s]))
        yield
        for e in (1, -1, 2, -2, 3, -3, 4):
            B[e].wait_recv()
            spread(e)
            if e != 1 and e != 2 and e != 3:
                yield
        for e in (1, -1):
            N1[e].wait_recv()
            N2[e].wait_recv()
        for c in F:
            c.wait_recv()
        part(t, 0)
        yield
        for d in (1, 3, 2):
            for e in (0, 1, -1, 2, -2, 3, -3, 4):
                XB[e, d].wait_recv()
            part(t, d)

    def width_sum(a0, na, result):
        a = pl.ds(a0, na)
        P16[a] = PF[a, oc].astype(BF16)
        cm = sems.copy(P16.at[a], C1.at[a], cdev)
        yield
        cm.wait_recv()
        zm = {}
        for d in (3, 2, 1):
            j = (zl + d) % ZL
            SZ[d, a] = (PF[a, core, j] + C1[a, j].astype(F32)).astype(BF16)
            zm[d] = sems.copy(SZ.at[d, a], RZ.at[d, a], ldev[d])
        total = PF[a, core, zl] + C1[a, zl].astype(F32)
        PF[a, core, zl] = total
        yield
        for d in (1, 3, 2):
            zm[d].wait_recv()
            total = total + RZ[d, a].astype(F32)
        PF[a, core, zl] = total
        result()

    def width_gather(a0, na):
        a = pl.ds(a0, na)
        own = H.at[a, core, zl]
        zm = {d: sems.copy(own, own, ldev[d]) for d in (3, 2, 1)}
        cm = {0: sems.copy(own, own, cdev)}
        yield
        for d in (1, 3, 2):
            zm[d].wait_recv()
            piece = H.at[a, core, (zl + ZL - d) % ZL]
            cm[d] = sems.copy(piece, piece, cdev)
        yield
        for d in (0, 1, 3, 2):
            cm[d].wait_recv()

    def make_hidden():
        g, u = PF[0, core, zl], PF[1, core, zl]
        s = 1.0 / (1.0 + jnp.exp(-g))
        H[0, core, zl] = (g * s * u).astype(BF16)

    def make_grads():
        g, u, h = PF[0, core, zl], PF[1, core, zl], PF[2, core, zl]
        s = 1.0 / (1.0 + jnp.exp(-g))
        H[1, core, zl] = (h * u * s * (1.0 + g * (1.0 - s))).astype(BF16)
        H[2, core, zl] = (h * g * s).astype(BF16)

    def scatter_a(t):
        halves = {1: pl.ds(0, X // 2), -1: pl.ds(X // 2, X // 2)}
        F4, M = {}, {}

        def send(i, v, device):
            SA[t, i] = v.astype(BF16)
            M[i] = sems.copy(SA.at[t, i], RA.at[t, i], device)

        for i, s in enumerate((1, -1)):
            SF[t, i] = OT[t, halves[s], zh, ys(4)].astype(BF16)
            F4[i] = sems.copy(SF.at[t, i], RF.at[t, i], ydev[2 * s])
            send(i, OT[t, :, zh, ys(3 * s)], ydev[s])
        yield
        for i, s in enumerate((1, -1)):
            send(2 + i, OT[t, :, zh, ys(s)], ydev[s])
        yield
        for i, s in enumerate((1, -1)):
            M[i].wait_recv()
            F4[i].wait_recv()
            OT[t, halves[s], zh, ys(2 * s)] += RF[t, i].astype(F32)
            send(4 + i, OT[t, :, zh, ys(2 * s)] + RA[t, i].astype(F32), ydev[2 * s])
        yield
        v = OT[t, :, zh, y]
        for i in (2, 3, 4, 5):
            M[i].wait_recv()
            v = v + RA[t, i].astype(F32)
        SX[t] = v[1:].astype(BF16)
        xm = {d: sems.copy(SX.at[t, d - 1], RX.at[t, d - 1], xdev[d]) for d in (2, 1, 3)}
        ACC[t] = v[0]
        yield
        for d in (1, 3, 2):
            xm[d].wait_recv()
            ACC[t] += RX[t, d - 1].astype(F32)

    def scatter_b(t):
        order = (4, -3, 3, -2, 2, -1, 1, 0)
        groups = ((0, 3), (3, 5), (5, 8))
        D, M = {}, {}
        for lo, hi in groups:
            for n in range(lo, hi):
                SD[t, :, n] = OT[t, pl.ds(1, X - 1), oz, ys(order[n])].astype(BF16)
            for d in (2, 1, 3):
                at = (t, d - 1, pl.ds(lo, hi - lo))
                D[lo, d] = sems.copy(SD.at[at], RD.at[at], xdev[d])
        yield
        for lo, hi in groups:
            for d in (1, 3, 2):
                D[lo, d].wait_recv()
            for n in range(lo, hi):
                v = OT[t, 0, oz, ys(order[n])]
                for d in range(1, X):
                    v = v + RD[t, d - 1, n].astype(F32)
                if order[n]:
                    SY[t, n] = v.astype(BF16)
                    M[n] = sems.copy(SY.at[t, n], RY.at[t, n], ydev[order[n]])
            yield
        for n in (5, 6, 3, 4, 1, 2, 0):
            M[n].wait_recv()
            v = v + RY[t, n].astype(F32)
        SW[t] = v.astype(BF16)
        M[7] = sems.copy(SW.at[t], RW.at[t], zdev)
        yield
        M[7].wait_recv()

    def hid(i):
        return H[i].reshape(dw.shape[0], T)

    def grads():
        for d in range(X):
            i = xs(-d)
            dwg[:, cols(i)] = mm(hid(0), block(1, d), (1, 1))
            yield
            gwg[cols(i), :] = mm(block(0, d), hid(1), (1, 1))
            yield
            uwg[cols(i), :] = mm(block(0, d), hid(2), (1, 1))
            yield

    def put(t, d, v):
        OT[t, d] = v.reshape(ZH, Y, 16, T)

    def drain(g):
        for _ in g:
            pass

    both = G.at[:, 0, zh, y]
    zm = sems.copy(both, both, zdev)
    tok, cot = gather(0, zm), gather(1, zm)
    left = True
    while left:
        left = False
        for _ in tok:
            left = True
            break
        if left:
            next(cot)
    pre = width_sum(0, 2, make_hidden)
    next(pre)
    next(pre)
    drain(cot)
    post = width_sum(2, 1, make_grads)
    next(post)
    next(post)
    drain(pre)
    fore = width_gather(0, 1)
    next(fore)
    drain(post)
    back = width_gather(1, 2)
    next(back)
    drain(fore)
    for d in range(X):
        put(0, d, mm(dwT[xs(d)], hid(0), (1, 0)))
    out = [scatter_b(0), scatter_a(0)]
    for g in out:
        next(g)
    drain(back)
    for d in range(X):
        i = xs(d)
        put(1, d, mm(gw[cols(i), :], hid(1), (1, 0)) + mm(uw[cols(i), :], hid(2), (1, 0)))
    turns(scatter_b(1), scatter_a(1), *out, grads())
    stores = []

    def store(src, dst):
        c = pltpu.make_async_copy(src, dst, local_sem.at[5 + len(stores)])
        c.start()
        stores.append(c)

    for src, dst in ((dwg, dwg_hbm), (gwg, gwg_hbm), (uwg, uwg_hbm)):
        store(src, dst)
    for t, ref in enumerate((out_hbm, inp_hbm)):
        io[t] = (ACC[t] + RW[t].astype(F32)).astype(BF16)[:, :tokens]
        store(io.at[t], ref)
    for c in sems.live:
        c.wait_send()
    for c in stores:
        c.wait()
    assert sems.used <= send_sem.shape[0], sems.used


def hand_on(*refs):
    n = (len(refs) - 1) // 3
    src, dst, via, sem = refs[:n], refs[n : 2 * n], refs[2 * n : 3 * n], refs[-1]
    ins = [pltpu.make_async_copy(src[i], via[i], sem.at[0, i]) for i in range(n)]
    outs = [pltpu.make_async_copy(via[i], dst[i], sem.at[1, i]) for i in range(n)]
    for c in ins:
        c.start()
    for i, c in enumerate(ins):
        c.wait()
        outs[i].start()
    for c in outs:
        c.wait()


def body(tokens, gate_weight, up_weight, down_weight, cotangent):
    n, (depth, hidden) = tokens.shape[0], gate_weight.shape
    T = -(-n // 128) * 128
    V = pltpu.VMEM
    part, span = hidden // (CORES * ZL), ZH * Y * 16
    scratch = [
        V((2, 16, n), BF16),
        V(gate_weight.shape, BF16), V(up_weight.shape, BF16), V(down_weight.shape, BF16),
        V((X, hidden, span), BF16), V((X, hidden, span), BF16), V((X, span, hidden), BF16),
        V(gate_weight.shape, F32), V(up_weight.shape, F32), V(down_weight.shape, F32),
        V((2, X, ZH, Y, 16, T), BF16),
        V((3, CORES, ZL, part, T), F32),
        V((3, ZL, part, T), BF16), V((3, ZL, part, T), BF16),
        V((ZL, 3, part, T), BF16), V((ZL, 3, part, T), BF16),
        V((3, CORES, ZL, part, T), BF16),
        V((2, X, ZH, Y, 16, T), F32),
        V((2, 6, X, 16, T), BF16), V((2, 6, X, 16, T), BF16),
        V((2, 2, X // 2, 16, T), BF16), V((2, 2, X // 2, 16, T), BF16),
        V((2, X - 1, 16, T), BF16), V((2, X - 1, 16, T), BF16),
        V((2, 16, T), F32),
        V((2, X - 1, Y, 16, T), BF16), V((2, X - 1, Y, 16, T), BF16),
        V((2, Y, 16, T), BF16), V((2, Y, 16, T), BF16),
        V((2, 16, T), BF16), V((2, 16, T), BF16),
        pltpu.SemaphoreType.DMA((200,)),
        pltpu.SemaphoreType.DMA((200,)),
        pltpu.SemaphoreType.DMA((10,)),
    ]
    anywhere = pl.BlockSpec(memory_space=pl.ANY)
    S = jax.ShapeDtypeStruct
    shapes = (
        S((16, n), BF16), S((16, n), BF16),
        S(gate_weight.shape, F32), S(up_weight.shape, F32), S(down_weight.shape, F32),
    )
    outs = pl.pallas_call(
        kernel,
        out_shape=shapes,
        in_specs=[anywhere] * 5,
        out_specs=(anywhere,) * 5,
        scratch_shapes=scratch,
        compiler_params=pltpu.CompilerParams(
            collective_id=0, has_side_effects=True, vmem_limit_bytes=60 * 2**20
        ),
        cost_estimate=pl.CostEstimate(flops=18 * n * depth * hidden, bytes_accessed=18 * depth * hidden, transcendentals=0),
        name="ffn",
    )(tokens.T, cotangent.T, gate_weight, up_weight, down_weight)
    output, input_grad, *grads = pl.pallas_call(
        hand_on,
        out_shape=shapes,
        in_specs=[anywhere] * 5,
        out_specs=(anywhere,) * 5,
        scratch_shapes=[V(a.shape, a.dtype) for a in shapes] + [pltpu.SemaphoreType.DMA((2, len(shapes)))],
        compiler_params=pltpu.CompilerParams(vmem_limit_bytes=60 * 2**20),
        name="hand_on",
    )(*outs)
    return (output.T, input_grad.T, *grads)


def solution(mesh):
    return jax.shard_map(
        body,
        mesh=mesh,
        in_specs=(
            P(None, ("width", "blk")),
            P("width", "blk"),
            P("width", "blk"),
            P("blk", "width"),
            P(None, ("width", "blk")),
        ),
        out_specs=(
            P(None, ("width", "blk")),
            P(None, ("width", "blk")),
            P("width", "blk"),
            P("width", "blk"),
            P("blk", "width"),
        ),
        check_vma=False,
    )
```

```python
import functools

import jax
import jax.numpy as jnp
from jax import lax
from jax.experimental import pallas as pl
from jax.experimental.pallas import tpu as pltpu
from jax.sharding import PartitionSpec as P

MESH = pl.DeviceIdType.MESH
X, ZH, Y = 4, 2, 8
ZL, CORES = 4, 2
F32, BF16 = jnp.float32, jnp.bfloat16
FAR = (4, 3, -3, 2, -2, 1, -1, 0)


def mm(left, right, dims):
    return lax.dot_general(left, right, ((dims[:1], dims[1:]), ((), ())), preferred_element_type=F32)


class Sems:
    def __init__(self, send, recv):
        self.send, self.recv, self.used, self.live = send, recv, 0, []

    def copy(self, src, dst, device):
        i = self.used
        self.used += 1
        c = pltpu.make_async_remote_copy(
            src_ref=src, dst_ref=dst, send_sem=self.send.at[i], recv_sem=self.recv.at[i],
            device_id=device, device_id_type=MESH,
        )
        c.start()
        self.live.append(c)
        return c

    def settle(self):
        for c in self.live:
            c.wait_send()
        self.live = []


def kernel(
    tok_hbm, cot_hbm, gw_hbm, uw_hbm, dw_hbm,
    out_hbm, inp_hbm, gwg_hbm, uwg_hbm, dwg_hbm,
    io, gw, uw, dw, wT, dwT, gwg, uwg, dwg, G, PF, P16, C1, SZ, RZ, H, OT,
    SA, RA, SF, RF, SX, RX, ACC, SD, RD, SY, RY, SUM,
    send_sem, recv_sem, local_sem,
):
    b, w = lax.axis_index("blk"), lax.axis_index("width")
    x, zh, y = b // (ZH * Y), (b // Y) % ZH, b % Y
    zl, core = w // CORES, w % CORES
    oz, oc = 1 - zh, 1 - core
    tokens = io.shape[-1]
    T = G.shape[-1]
    span = ZH * Y * 16

    def xs(d):
        return (x + d % X) % X

    def ys(d):
        return (y + d % Y) % Y

    xdev = {d: ((xs(d) * ZH + zh) * Y + y, w) for d in range(1, X)}
    ydev = {d: ((x * ZH + zh) * Y + ys(d), w) for d in (1, -1, 2, -2, 3, -3, 4)}
    zdev = {d: ((x * ZH + oz) * Y + ys(d), w) for d in FAR}
    cdev = (b, zl * CORES + oc)
    ldev = {d: (b, ((zl + d) % ZL) * CORES + core) for d in range(1, ZL)}

    barrier = pltpu.get_barrier_semaphore()
    partners = list(zdev.values()) + list(ldev.values()) + list(ydev.values()) + list(xdev.values()) + [cdev]
    for p in partners:
        pl.semaphore_signal(barrier, inc=1, device_id=p, device_id_type=MESH)

    loads = [
        pltpu.make_async_copy(s, d, local_sem.at[i])
        for i, (s, d) in enumerate(
            ((tok_hbm, io.at[0]), (cot_hbm, io.at[1]), (gw_hbm, gw), (uw_hbm, uw), (dw_hbm, dw))
        )
    ]
    for c in loads:
        c.start()
    for t in range(2):
        loads[t].wait()
        G[t, 0, zh, y] = jnp.pad(io[t].astype(F32), ((0, 0), (0, T - tokens))).astype(BF16)
    pl.semaphore_wait(barrier, len(partners))

    sems = Sems(send_sem, recv_sem)

    def cols(i):
        return pl.ds(pl.multiple_of(i * span, span), span)

    def block(t, d):
        return G[t, d].reshape(span, T)

    def parts(t):
        @pl.loop(0, X)
        def _(d):
            i = (x + X - d) % X
            for n in range(2) if t == 0 else (2,):
                left = wT[n, i] if t == 0 else dw[:, cols(i)]
                PF[n] += mm(left, block(t, d), (1, 0)).reshape(PF.shape[1:])

    def gather(t):
        own, rest = G.at[t, 0, zh, y], G.at[t, pl.ds(1, X - 1), zh, y]
        near = (2, -2, 1, -1)
        xm = {d: sems.copy(own, G.at[t, d, zh, y], xdev[d]) for d in (2, 1, 3)}
        B = {e: sems.copy(own, own, zdev[e]) for e in FAR}
        N1 = {e: sems.copy(own, own, ydev[e]) for e in near}
        XB, F = [], []
        yield
        for d in (1, 3, 2):
            xm[d].wait_recv()
        N2 = {e: sems.copy(rest, rest, ydev[e]) for e in near}
        yield
        for e in FAR:
            B[e].wait_recv()
            piece = G.at[t, 0, oz, ys(-e)]
            for d in (2, 1, 3):
                XB.append(sems.copy(piece, G.at[t, d, oz, ys(-e)], xdev[d]))
        yield
        for s, half in ((1, pl.ds(0, X // 2)), (-1, pl.ds(X // 2, X // 2))):
            N1[2 * s].wait_recv()
            N2[2 * s].wait_recv()
            piece = G.at[t, half, zh, ys(-2 * s)]
            F.append(sems.copy(piece, piece, ydev[2 * s]))
            piece = G.at[t, :, zh, ys(-2 * s)]
            F.append(sems.copy(piece, piece, ydev[s]))
        yield
        for e in (1, -1):
            N1[e].wait_recv()
            N2[e].wait_recv()
        for c in F + XB:
            c.wait_recv()
        parts(t)

    def width_sum(a0, na, result):
        a = pl.ds(a0, na)
        P16[a] = PF[a, oc].astype(BF16)
        cm = sems.copy(P16.at[a], C1.at[a], cdev)
        yield
        cm.wait_recv()
        zm = {}
        for d in (3, 2, 1):
            j = (zl + d) % ZL
            SZ[d, a] = (PF[a, core, j] + C1[a, j].astype(F32)).astype(BF16)
            zm[d] = sems.copy(SZ.at[d, a], RZ.at[d, a], ldev[d])
        total = PF[a, core, zl] + C1[a, zl].astype(F32)
        PF[a, core, zl] = total
        yield
        for d in (1, 3, 2):
            zm[d].wait_recv()
            total = total + RZ[d, a].astype(F32)
        PF[a, core, zl] = total
        result()

    def width_gather(a0, na):
        a = pl.ds(a0, na)
        own = H.at[a, core, zl]
        zm = {d: sems.copy(own, own, ldev[d]) for d in (3, 2, 1)}
        cm = {0: sems.copy(own, own, cdev)}
        yield
        for d in (1, 3, 2):
            zm[d].wait_recv()
            piece = H.at[a, core, (zl + ZL - d) % ZL]
            cm[d] = sems.copy(piece, piece, cdev)
        yield
        for d in (0, 1, 3, 2):
            cm[d].wait_recv()

    def make_hidden():
        g, u = PF[0, core, zl], PF[1, core, zl]
        s = 1.0 / (1.0 + jnp.exp(-g))
        H[0, core, zl] = (g * s * u).astype(BF16)

    def make_grads():
        g, u, h = PF[0, core, zl], PF[1, core, zl], PF[2, core, zl]
        s = 1.0 / (1.0 + jnp.exp(-g))
        H[1, core, zl] = (h * u * s * (1.0 + g * (1.0 - s))).astype(BF16)
        H[2, core, zl] = (h * g * s).astype(BF16)

    def scatter_a(t):
        halves = {1: pl.ds(0, X // 2), -1: pl.ds(X // 2, X // 2)}
        F4, M = {}, {}

        def send(i, v, device):
            SA[t, i] = v.astype(BF16)
            M[i] = sems.copy(SA.at[t, i], RA.at[t, i], device)

        for i, s in enumerate((1, -1)):
            SF[t, i] = OT[t, halves[s], zh, ys(4)].astype(BF16)
            F4[i] = sems.copy(SF.at[t, i], RF.at[t, i], ydev[2 * s])
            send(i, OT[t, :, zh, ys(3 * s)], ydev[s])
        for i, s in enumerate((1, -1)):
            send(2 + i, OT[t, :, zh, ys(s)], ydev[s])
        yield
        for i, s in enumerate((1, -1)):
            M[i].wait_recv()
            F4[i].wait_recv()
            OT[t, halves[s], zh, ys(2 * s)] += RF[t, i].astype(F32)
            send(4 + i, OT[t, :, zh, ys(2 * s)] + RA[t, i].astype(F32), ydev[2 * s])
        yield
        v = OT[t, :, zh, y]
        for i in (2, 3, 4, 5):
            M[i].wait_recv()
            v = v + RA[t, i].astype(F32)
        SX[t] = v[1:].astype(BF16)
        xm = {d: sems.copy(SX.at[t, d - 1], RX.at[t, d - 1], xdev[d]) for d in (2, 1, 3)}
        ACC[t] = v[0]
        yield
        for d in (1, 3, 2):
            xm[d].wait_recv()
            ACC[t] += RX[t, d - 1].astype(F32)

    def scatter_b(t):
        groups = ((0, 3), (3, 5), (5, 8))
        D, M = {}, []
        for lo, hi in groups:
            for n in range(lo, hi):
                SD[t, :, n] = OT[t, pl.ds(1, X - 1), oz, ys(FAR[n])].astype(BF16)
            for d in (2, 1, 3):
                at = (t, d - 1, pl.ds(lo, hi - lo))
                D[lo, d] = sems.copy(SD.at[at], RD.at[at], xdev[d])
        yield
        for lo, hi in groups:
            for d in (1, 3, 2):
                D[lo, d].wait_recv()
            for n in range(lo, hi):
                v = OT[t, 0, oz, ys(FAR[n])]
                for d in range(1, X):
                    v = v + RD[t, d - 1, n].astype(F32)
                SY[t, n] = v.astype(BF16)
                M.append(sems.copy(SY.at[t, n], RY.at[t, n], zdev[FAR[n]]))
            yield
        v = None
        for n in range(Y):
            M[n].wait_recv()
            v = RY[t, n].astype(F32) + (0.0 if v is None else v)
        SUM[t] = v

    def hid(i):
        return H[i].reshape(dw.shape[0], T)

    stores = []

    def store(src, dst):
        c = pltpu.make_async_copy(src, dst, local_sem.at[5 + len(stores)])
        c.start()
        stores.append(c)

    def grads():
        for n, (g, g_hbm) in enumerate(((gwg, gwg_hbm), (uwg, uwg_hbm))):

            @pl.loop(0, X)
            def _(d):
                g[cols((x + X - d) % X), :] = mm(block(0, d), hid(1 + n), (1, 1))

            store(g, g_hbm)
            yield

    def put(t, d, v):
        OT[t, d] = v.reshape(ZH, Y, 16, T)

    def drain(g):
        for _ in g:
            pass

    tok, cot = gather(0), gather(1)
    next(tok)
    next(cot)
    for c in loads[2:]:
        c.wait()
    PF[...] = jnp.zeros_like(PF)

    @pl.loop(0, X)
    def _(i):
        wT[0, i] = gw[cols(i), :].T
        wT[1, i] = uw[cols(i), :].T
        dwT[i] = dw[:, cols(i)].T

    for g in (tok, cot, tok, tok, cot, cot):
        next(g)
    drain(tok)
    pre = width_sum(0, 2, make_hidden)
    next(pre)
    next(pre)
    drain(cot)
    post = width_sum(2, 1, make_grads)
    next(post)
    next(post)
    sems.settle()
    drain(pre)
    fore = width_gather(0, 1)
    next(fore)
    drain(post)
    back = width_gather(1, 2)
    next(back)
    drain(fore)

    @pl.loop(0, X)
    def _(d):
        put(0, d, mm(dwT[(x + d) % X], hid(0), (1, 0)))

    b0, a0, b1, a1, dw_up = scatter_b(0), scatter_a(0), scatter_b(1), scatter_a(1), grads()
    next(b0)
    next(a0)

    @pl.loop(0, X)
    def _(d):
        dwg[:, cols((x + X - d) % X)] = mm(hid(0), block(1, d), (1, 1))

    store(dwg, dwg_hbm)
    drain(back)

    @pl.loop(0, X)
    def _(d):
        i = (x + d) % X
        put(1, d, mm(gw[cols(i), :], hid(1), (1, 0)) + mm(uw[cols(i), :], hid(2), (1, 0)))

    for g in (b1, a1, b0, a0, b0, b0, b1, a1, b1, b1, dw_up, a0, dw_up, a1):
        next(g)
    for g in (dw_up, b0, a0, a1, b1):
        drain(g)
    for t, ref in enumerate((out_hbm, inp_hbm)):
        io[t] = (ACC[t] + SUM[t]).astype(BF16)[:, :tokens]
        store(io.at[t], ref)
    sems.settle()
    for c in stores:
        c.wait()
    assert sems.used <= send_sem.shape[0], sems.used


def hand_on(*refs):
    n = (len(refs) - 1) // 3
    src, dst, via, sem = refs[:n], refs[n : 2 * n], refs[2 * n : 3 * n], refs[-1]
    ins = [pltpu.make_async_copy(src[i], via[i], sem.at[0, i]) for i in range(n)]
    outs = [pltpu.make_async_copy(via[i], dst[i], sem.at[1, i]) for i in range(n)]
    for c in ins:
        c.start()
    for i, c in enumerate(ins):
        c.wait()
        outs[i].start()
    for c in outs:
        c.wait()


def body(tokens, gate_weight, up_weight, down_weight, cotangent):
    n, (depth, hidden) = tokens.shape[0], gate_weight.shape
    T = -(-n // 128) * 128
    V = pltpu.VMEM
    part, span = hidden // (CORES * ZL), ZH * Y * 16
    scratch = [
        V((2, 16, n), BF16),
        V(gate_weight.shape, BF16), V(up_weight.shape, BF16), V(down_weight.shape, BF16),
        V((2, X, hidden, span), BF16), V((X, span, hidden), BF16),
        V(gate_weight.shape, F32), V(up_weight.shape, F32), V(down_weight.shape, F32),
        V((2, X, ZH, Y, 16, T), BF16),
        V((3, CORES, ZL, part, T), F32),
        V((3, ZL, part, T), BF16), V((3, ZL, part, T), BF16),
        V((ZL, 3, part, T), BF16), V((ZL, 3, part, T), BF16),
        V((3, CORES, ZL, part, T), BF16),
        V((2, X, ZH, Y, 16, T), F32),
        V((2, 6, X, 16, T), BF16), V((2, 6, X, 16, T), BF16),
        V((2, 2, X // 2, 16, T), BF16), V((2, 2, X // 2, 16, T), BF16),
        V((2, X - 1, 16, T), BF16), V((2, X - 1, 16, T), BF16),
        V((2, 16, T), F32),
        V((2, X - 1, Y, 16, T), BF16), V((2, X - 1, Y, 16, T), BF16),
        V((2, Y, 16, T), BF16), V((2, Y, 16, T), BF16),
        V((2, 16, T), F32),
        pltpu.SemaphoreType.DMA((200,)),
        pltpu.SemaphoreType.DMA((200,)),
        pltpu.SemaphoreType.DMA((10,)),
    ]
    anywhere = pl.BlockSpec(memory_space=pl.ANY)
    S = jax.ShapeDtypeStruct
    shapes = (
        S((16, n), BF16), S((16, n), BF16),
        S(gate_weight.shape, F32), S(up_weight.shape, F32), S(down_weight.shape, F32),
    )
    outs = pl.pallas_call(
        kernel,
        out_shape=shapes,
        in_specs=[anywhere] * 5,
        out_specs=(anywhere,) * 5,
        scratch_shapes=scratch,
        compiler_params=pltpu.CompilerParams(
            collective_id=0, has_side_effects=True, vmem_limit_bytes=60 * 2**20
        ),
        cost_estimate=pl.CostEstimate(flops=18 * n * depth * hidden, bytes_accessed=18 * depth * hidden, transcendentals=0),
        name="ffn",
    )(tokens.T, cotangent.T, gate_weight, up_weight, down_weight)
    output, input_grad, *grads = pl.pallas_call(
        hand_on,
        out_shape=shapes,
        in_specs=[anywhere] * 5,
        out_specs=(anywhere,) * 5,
        scratch_shapes=[V(a.shape, a.dtype) for a in shapes] + [pltpu.SemaphoreType.DMA((2, len(shapes)))],
        compiler_params=pltpu.CompilerParams(vmem_limit_bytes=60 * 2**20),
        name="hand_on",
    )(*outs)
    return (output.T, input_grad.T, *grads)


def solution(mesh):
    return jax.shard_map(
        body,
        mesh=mesh,
        in_specs=(
            P(None, ("width", "blk")),
            P("width", "blk"),
            P("width", "blk"),
            P("blk", "width"),
            P(None, ("width", "blk")),
        ),
        out_specs=(
            P(None, ("width", "blk")),
            P(None, ("width", "blk")),
            P("width", "blk"),
            P("width", "blk"),
            P("blk", "width"),
        ),
        check_vma=False,
    )
```

```python
import functools

import jax
import jax.numpy as jnp
from jax import lax
from jax.experimental import pallas as pl
from jax.experimental.pallas import tpu as pltpu
from jax.sharding import PartitionSpec as P

MESH = pl.DeviceIdType.MESH
PIECES = 4
X, ZH, Y = 4, 2, 8
ZL, CORES = 4, 2
F32, BF16 = jnp.float32, jnp.bfloat16
FAR = (4, 3, -3, 2, -2, 1, -1, 0)


def mm(left, right, dims):
    return lax.dot_general(left, right, ((dims[:1], dims[1:]), ((), ())), preferred_element_type=F32)


class Sems:
    def __init__(self, send, recv):
        self.send, self.recv, self.used, self.live = send, recv, 0, []

    def copy(self, src, dst, device):
        i = self.used
        self.used += 1
        c = pltpu.make_async_remote_copy(
            src_ref=src, dst_ref=dst, send_sem=self.send.at[i], recv_sem=self.recv.at[i],
            device_id=device, device_id_type=MESH,
        )
        c.start()
        self.live.append(c)
        return c

    def settle(self):
        for c in self.live:
            c.wait_send()
        self.live = []


def kernel(
    tok_hbm, cot_hbm, gw_hbm, uw_hbm, dw_hbm,
    out_hbm, inp_hbm, gwg_hbm, uwg_hbm, dwg_hbm,
    io, gw, uw, dw, wT, dwT, gwg, uwg, dwg, G, PF, P16, C1, SZ, RZ, H, OT,
    SA, RA, SF, RF, SX, RX, ACC, SD, RD, SY, RY, SUM,
    send_sem, recv_sem, local_sem,
):
    b, w = lax.axis_index("blk"), lax.axis_index("width")
    x, zh, y = b // (ZH * Y), (b // Y) % ZH, b % Y
    zl, core = w // CORES, w % CORES
    oz, oc = 1 - zh, 1 - core
    tokens = io.shape[-1]
    T = G.shape[-1]
    span = ZH * Y * 16

    def xs(d):
        return (x + d % X) % X

    def ys(d):
        return (y + d % Y) % Y

    xdev = {d: ((xs(d) * ZH + zh) * Y + y, w) for d in range(1, X)}
    ydev = {d: ((x * ZH + zh) * Y + ys(d), w) for d in (1, -1, 2, -2, 3, -3, 4)}
    zdev = {d: ((x * ZH + oz) * Y + ys(d), w) for d in FAR}
    cdev = (b, zl * CORES + oc)
    ldev = {d: (b, ((zl + d) % ZL) * CORES + core) for d in range(1, ZL)}

    barrier = pltpu.get_barrier_semaphore()
    partners = list(zdev.values()) + list(ldev.values()) + list(ydev.values()) + list(xdev.values()) + [cdev]
    for p in partners:
        pl.semaphore_signal(barrier, inc=1, device_id=p, device_id_type=MESH)

    loads = [
        pltpu.make_async_copy(s, d, local_sem.at[i])
        for i, (s, d) in enumerate(
            ((tok_hbm, io.at[0]), (cot_hbm, io.at[1]), (gw_hbm, gw), (uw_hbm, uw), (dw_hbm, dw))
        )
    ]
    for c in loads:
        c.start()
    for t in range(2):
        loads[t].wait()
        G[t, 0, zh, y] = jnp.pad(io[t].astype(F32), ((0, 0), (0, T - tokens))).astype(BF16)
    pl.semaphore_wait(barrier, len(partners))

    sems = Sems(send_sem, recv_sem)

    def cols(i):
        return pl.ds(pl.multiple_of(i * span, span), span)

    def block(t, d):
        return G[t, d].reshape(span, T)

    def parts(t):
        @pl.loop(0, X)
        def _(d):
            i = (x + X - d) % X
            for n in range(2) if t == 0 else (2,):
                left = wT[n, i] if t == 0 else dw[:, cols(i)]
                PF[n] += mm(left, block(t, d), (1, 0)).reshape(PF.shape[1:])

    def gather(t):
        own, line = G.at[t, 0, zh, y], G.at[t, :, zh, y]
        near = (2, -2, 1, -1)
        xm = {d: sems.copy(own, G.at[t, d, zh, y], xdev[d]) for d in (2, 1, 3)}
        B = {e: sems.copy(own, own, zdev[e]) for e in FAR}
        XB, F = [], []
        yield
        for d in (1, 3, 2):
            xm[d].wait_recv()
        N = {e: sems.copy(line, line, ydev[e]) for e in near}
        yield
        for e in FAR:
            B[e].wait_recv()
            piece = G.at[t, 0, oz, ys(-e)]
            for d in (2, 1, 3):
                XB.append(sems.copy(piece, G.at[t, d, oz, ys(-e)], xdev[d]))
        yield
        for s, half in ((1, pl.ds(0, X // 2)), (-1, pl.ds(X // 2, X // 2))):
            N[2 * s].wait_recv()
            piece = G.at[t, half, zh, ys(-2 * s)]
            F.append(sems.copy(piece, piece, ydev[2 * s]))
            piece = G.at[t, :, zh, ys(-2 * s)]
            F.append(sems.copy(piece, piece, ydev[s]))
        yield
        for e in (1, -1):
            N[e].wait_recv()
        for c in F + XB:
            c.wait_recv()
        parts(t)

    def width_sum(a0, na, result):
        a = pl.ds(a0, na)
        P16[a] = PF[a, oc].astype(BF16)
        cm = sems.copy(P16.at[a], C1.at[a], cdev)
        yield
        cm.wait_recv()
        zm = {}
        for d in (3, 2, 1):
            j = (zl + d) % ZL
            SZ[d, a] = (PF[a, core, j] + C1[a, j].astype(F32)).astype(BF16)
            zm[d] = sems.copy(SZ.at[d, a], RZ.at[d, a], ldev[d])
        total = PF[a, core, zl] + C1[a, zl].astype(F32)
        PF[a, core, zl] = total
        yield
        for d in (1, 3, 2):
            zm[d].wait_recv()
            total = total + RZ[d, a].astype(F32)
        PF[a, core, zl] = total
        result()

    def width_gather(a0, na):
        a = pl.ds(a0, na)
        own = H.at[a, core, zl]
        zm = {d: sems.copy(own, own, ldev[d]) for d in (3, 2, 1)}
        cm = {0: sems.copy(own, own, cdev)}
        yield
        for d in (1, 3, 2):
            zm[d].wait_recv()
            piece = H.at[a, core, (zl + ZL - d) % ZL]
            cm[d] = sems.copy(piece, piece, cdev)
        yield
        for d in (0, 1, 3, 2):
            cm[d].wait_recv()

    def make_hidden():
        g, u = PF[0, core, zl], PF[1, core, zl]
        s = 1.0 / (1.0 + jnp.exp(-g))
        H[0, core, zl] = (g * s * u).astype(BF16)

    def make_grads():
        g, u, h = PF[0, core, zl], PF[1, core, zl], PF[2, core, zl]
        s = 1.0 / (1.0 + jnp.exp(-g))
        H[1, core, zl] = (h * u * s * (1.0 + g * (1.0 - s))).astype(BF16)
        H[2, core, zl] = (h * g * s).astype(BF16)

    def scatter_a(t):
        halves = {1: pl.ds(0, X // 2), -1: pl.ds(X // 2, X // 2)}
        F4, M = {}, {}

        def send(i, v, device):
            SA[t, i] = v.astype(BF16)
            M[i] = sems.copy(SA.at[t, i], RA.at[t, i], device)

        for i, s in enumerate((1, -1)):
            SF[t, i] = OT[t, halves[s], zh, ys(4)].astype(BF16)
            F4[i] = sems.copy(SF.at[t, i], RF.at[t, i], ydev[2 * s])
            send(i, OT[t, :, zh, ys(3 * s)], ydev[s])
        for i, s in enumerate((1, -1)):
            send(2 + i, OT[t, :, zh, ys(s)], ydev[s])
        yield
        for i, s in enumerate((1, -1)):
            M[i].wait_recv()
            F4[i].wait_recv()
            OT[t, halves[s], zh, ys(2 * s)] += RF[t, i].astype(F32)
            send(4 + i, OT[t, :, zh, ys(2 * s)] + RA[t, i].astype(F32), ydev[2 * s])
        yield
        v = OT[t, :, zh, y]
        for i in (2, 3, 4, 5):
            M[i].wait_recv()
            v = v + RA[t, i].astype(F32)
        SX[t] = v[1:].astype(BF16)
        xm = {d: sems.copy(SX.at[t, d - 1], RX.at[t, d - 1], xdev[d]) for d in (2, 1, 3)}
        ACC[t] = v[0]
        yield
        for d in (1, 3, 2):
            xm[d].wait_recv()
            ACC[t] += RX[t, d - 1].astype(F32)

    def scatter_b(t):
        groups = ((0, 4), (4, 8))
        D, M = {}, []
        for lo, hi in groups:
            for n in range(lo, hi):
                SD[t, :, n] = OT[t, pl.ds(1, X - 1), oz, ys(FAR[n])].astype(BF16)
            for d in (2, 1, 3):
                at = (t, d - 1, pl.ds(lo, hi - lo))
                D[lo, d] = sems.copy(SD.at[at], RD.at[at], xdev[d])
        yield
        for lo, hi in groups:
            for d in (1, 3, 2):
                D[lo, d].wait_recv()
            for n in range(lo, hi):
                v = OT[t, 0, oz, ys(FAR[n])]
                for d in range(1, X):
                    v = v + RD[t, d - 1, n].astype(F32)
                SY[t, n] = v.astype(BF16)
                M.append(sems.copy(SY.at[t, n], RY.at[t, n], zdev[FAR[n]]))
            yield
        v = None
        for n in range(Y):
            M[n].wait_recv()
            v = RY[t, n].astype(F32) + (0.0 if v is None else v)
        SUM[t] = v

    def hid(i):
        return H[i].reshape(dw.shape[0], T)

    stores = []

    def store(src, dst):
        c = pltpu.make_async_copy(src, dst, local_sem.at[5 + len(stores)])
        c.start()
        stores.append(c)

    def grads():
        for n, (g, g_hbm) in enumerate(((gwg, gwg_hbm), (uwg, uwg_hbm))):

            @pl.loop(0, X)
            def _(d):
                g[cols((x + X - d) % X), :] = mm(block(0, d), hid(1 + n), (1, 1))

            store(g, g_hbm)
            yield

    def put(t, d, v):
        OT[t, d] = v.reshape(ZH, Y, 16, T)

    def drain(g):
        for _ in g:
            pass

    tok, cot = gather(0), gather(1)
    next(tok)
    next(cot)
    for c in loads[2:]:
        c.wait()
    PF[...] = jnp.zeros_like(PF)

    @pl.loop(0, X)
    def _(i):
        wT[0, i] = gw[cols(i), :].T
        wT[1, i] = uw[cols(i), :].T
        dwT[i] = dw[:, cols(i)].T

    for g in (tok, cot, tok, tok, cot, cot):
        next(g)
    drain(tok)
    pre = width_sum(0, 2, make_hidden)
    next(pre)
    next(pre)
    drain(cot)
    post = width_sum(2, 1, make_grads)
    next(post)
    next(post)
    sems.settle()
    drain(pre)
    fore = width_gather(0, 1)
    next(fore)
    drain(post)
    back = width_gather(1, 2)
    next(back)
    drain(fore)

    @pl.loop(0, X)
    def _(d):
        put(0, d, mm(dwT[(x + d) % X], hid(0), (1, 0)))

    b0, a0, b1, a1, dw_up = scatter_b(0), scatter_a(0), scatter_b(1), scatter_a(1), grads()
    next(b0)
    next(a0)

    @pl.loop(0, X)
    def _(d):
        dwg[:, cols((x + X - d) % X)] = mm(hid(0), block(1, d), (1, 1))

    store(dwg, dwg_hbm)
    drain(back)

    @pl.loop(0, X)
    def _(d):
        i = (x + d) % X
        put(1, d, mm(gw[cols(i), :], hid(1), (1, 0)) + mm(uw[cols(i), :], hid(2), (1, 0)))

    for g in (b1, a1, b0, a0, b0, b1, a1, b1, dw_up, a0, dw_up, a1):
        next(g)
    sems.settle()
    for g in (dw_up, a0, b0, a1, b1):
        drain(g)
    for t, ref in enumerate((out_hbm, inp_hbm)):
        io[t] = (ACC[t] + SUM[t]).astype(BF16)[:, :tokens]
        store(io.at[t], ref)
    sems.settle()
    for c in stores:
        c.wait()
    assert sems.used <= send_sem.shape[0], sems.used


def hand_on(*refs):
    n = (len(refs) - 1) // 3
    src, dst, via, sem = refs[:n], refs[n : 2 * n], refs[2 * n : 3 * n], refs[-1]
    ins, outs = [], []
    for i in range(n):
        rows = src[i].shape[0]
        step = max(16, rows // PIECES)
        for at in range(0, rows, step):
            s, k = pl.ds(at, step), len(ins)
            ins.append(pltpu.make_async_copy(src[i].at[s], via[i].at[s], sem.at[0, k]))
            outs.append(pltpu.make_async_copy(via[i].at[s], dst[i].at[s], sem.at[1, k]))
    for c in ins:
        c.start()
    for i, c in enumerate(ins):
        c.wait()
        outs[i].start()
    for c in outs:
        c.wait()


def body(tokens, gate_weight, up_weight, down_weight, cotangent):
    n, (depth, hidden) = tokens.shape[0], gate_weight.shape
    T = -(-n // 128) * 128
    V = pltpu.VMEM
    part, span = hidden // (CORES * ZL), ZH * Y * 16
    scratch = [
        V((2, 16, n), BF16),
        V(gate_weight.shape, BF16), V(up_weight.shape, BF16), V(down_weight.shape, BF16),
        V((2, X, hidden, span), BF16), V((X, span, hidden), BF16),
        V(gate_weight.shape, F32), V(up_weight.shape, F32), V(down_weight.shape, F32),
        V((2, X, ZH, Y, 16, T), BF16),
        V((3, CORES, ZL, part, T), F32),
        V((3, ZL, part, T), BF16), V((3, ZL, part, T), BF16),
        V((ZL, 3, part, T), BF16), V((ZL, 3, part, T), BF16),
        V((3, CORES, ZL, part, T), BF16),
        V((2, X, ZH, Y, 16, T), F32),
        V((2, 6, X, 16, T), BF16), V((2, 6, X, 16, T), BF16),
        V((2, 2, X // 2, 16, T), BF16), V((2, 2, X // 2, 16, T), BF16),
        V((2, X - 1, 16, T), BF16), V((2, X - 1, 16, T), BF16),
        V((2, 16, T), F32),
        V((2, X - 1, Y, 16, T), BF16), V((2, X - 1, Y, 16, T), BF16),
        V((2, Y, 16, T), BF16), V((2, Y, 16, T), BF16),
        V((2, 16, T), F32),
        pltpu.SemaphoreType.DMA((200,)),
        pltpu.SemaphoreType.DMA((200,)),
        pltpu.SemaphoreType.DMA((10,)),
    ]
    anywhere = pl.BlockSpec(memory_space=pl.ANY)
    S = jax.ShapeDtypeStruct
    shapes = (
        S((16, n), BF16), S((16, n), BF16),
        S(gate_weight.shape, F32), S(up_weight.shape, F32), S(down_weight.shape, F32),
    )
    outs = pl.pallas_call(
        kernel,
        out_shape=shapes,
        in_specs=[anywhere] * 5,
        out_specs=(anywhere,) * 5,
        scratch_shapes=scratch,
        compiler_params=pltpu.CompilerParams(
            collective_id=0, has_side_effects=True, vmem_limit_bytes=60 * 2**20
        ),
        cost_estimate=pl.CostEstimate(flops=18 * n * depth * hidden, bytes_accessed=18 * depth * hidden, transcendentals=0),
        name="ffn",
    )(tokens.T, cotangent.T, gate_weight, up_weight, down_weight)
    output, input_grad, *grads = pl.pallas_call(
        hand_on,
        out_shape=shapes,
        in_specs=[anywhere] * 5,
        out_specs=(anywhere,) * 5,
        scratch_shapes=[V(a.shape, a.dtype) for a in shapes] + [pltpu.SemaphoreType.DMA((2, PIECES * len(shapes)))],
        compiler_params=pltpu.CompilerParams(vmem_limit_bytes=60 * 2**20),
        name="hand_on",
    )(*outs)
    return (output.T, input_grad.T, *grads)


def solution(mesh):
    return jax.shard_map(
        body,
        mesh=mesh,
        in_specs=(
            P(None, ("width", "blk")),
            P("width", "blk"),
            P("width", "blk"),
            P("blk", "width"),
            P(None, ("width", "blk")),
        ),
        out_specs=(
            P(None, ("width", "blk")),
            P(None, ("width", "blk")),
            P("width", "blk"),
            P("width", "blk"),
            P("blk", "width"),
        ),
        check_vma=False,
    )
```

```python
import functools

import jax
import jax.numpy as jnp
from jax import lax
from jax.experimental import pallas as pl
from jax.experimental.pallas import tpu as pltpu
from jax.sharding import PartitionSpec as P

MESH = pl.DeviceIdType.MESH
PIECES = 4
X, ZH, Y = 4, 2, 8
ZL, CORES = 4, 2
F32, BF16 = jnp.float32, jnp.bfloat16
FAR = (4, 3, -3, 2, -2, 1, -1, 0)


def mm(left, right, dims):
    return lax.dot_general(left, right, ((dims[:1], dims[1:]), ((), ())), preferred_element_type=F32)


class Sems:
    def __init__(self, send, recv):
        self.send, self.recv, self.used, self.live = send, recv, 0, []

    def copy(self, src, dst, device):
        i = self.used
        self.used += 1
        c = pltpu.make_async_remote_copy(
            src_ref=src, dst_ref=dst, send_sem=self.send.at[i], recv_sem=self.recv.at[i],
            device_id=device, device_id_type=MESH,
        )
        c.start()
        self.live.append(c)
        return c

    def settle(self):
        for c in self.live:
            c.wait_send()
        self.live = []


def kernel(
    tok_hbm, cot_hbm, gw_hbm, uw_hbm, dw_hbm,
    out_hbm, inp_hbm, gwg_hbm, uwg_hbm, dwg_hbm,
    io, gw, uw, dw, wT, dwT, gwg, uwg, dwg, G, PF, P16, C1, SZ, RZ, H, OT,
    SA, RA, SF, RF, SX, RX, ACC, SD, RD, SY, RY, SUM,
    send_sem, recv_sem, local_sem,
):
    b, w = lax.axis_index("blk"), lax.axis_index("width")
    x, zh, y = b // (ZH * Y), (b // Y) % ZH, b % Y
    zl, core = w // CORES, w % CORES
    oz, oc = 1 - zh, 1 - core
    tokens = io.shape[-1]
    T = G.shape[-1]
    span = ZH * Y * 16

    def xs(d):
        return (x + d % X) % X

    def ys(d):
        return (y + d % Y) % Y

    xdev = {d: ((xs(d) * ZH + zh) * Y + y, w) for d in range(1, X)}
    ydev = {d: ((x * ZH + zh) * Y + ys(d), w) for d in (1, -1, 2, -2, 3, -3, 4)}
    zdev = {d: ((x * ZH + oz) * Y + ys(d), w) for d in FAR}
    cdev = (b, zl * CORES + oc)
    ldev = {d: (b, ((zl + d) % ZL) * CORES + core) for d in range(1, ZL)}

    barrier = pltpu.get_barrier_semaphore()
    partners = list(zdev.values()) + list(ldev.values()) + list(ydev.values()) + list(xdev.values()) + [cdev]
    for p in partners:
        pl.semaphore_signal(barrier, inc=1, device_id=p, device_id_type=MESH)

    loads = [
        pltpu.make_async_copy(s, d, local_sem.at[i])
        for i, (s, d) in enumerate(
            ((tok_hbm, io.at[0]), (cot_hbm, io.at[1]), (gw_hbm, gw), (uw_hbm, uw), (dw_hbm, dw))
        )
    ]
    for c in loads:
        c.start()
    for t in range(2):
        loads[t].wait()
        G[t, 0, zh, y] = jnp.pad(io[t].astype(F32), ((0, 0), (0, T - tokens))).astype(BF16)
    pl.semaphore_wait(barrier, len(partners))

    sems = Sems(send_sem, recv_sem)

    def cols(i):
        return pl.ds(pl.multiple_of(i * span, span), span)

    def block(t, d):
        return G[t, d].reshape(span, T)

    def parts(t):
        @pl.loop(0, X)
        def _(d):
            i = (x + X - d) % X
            for n in range(2) if t == 0 else (2,):
                left = wT[n, i] if t == 0 else dw[:, cols(i)]
                PF[n] += mm(left, block(t, d), (1, 0)).reshape(PF.shape[1:])

    def gather(t):
        own, line = G.at[t, 0, zh, y], G.at[t, :, zh, y]
        near = (2, -2, 1, -1)
        xm = {d: sems.copy(own, G.at[t, d, zh, y], xdev[d]) for d in (2, 1, 3)}
        B = {e: sems.copy(own, own, zdev[e]) for e in FAR}
        XB, F = [], []
        yield
        for d in (1, 3, 2):
            xm[d].wait_recv()
        N = {e: sems.copy(line, line, ydev[e]) for e in near}
        yield
        for e in FAR:
            B[e].wait_recv()
            piece = G.at[t, 0, oz, ys(-e)]
            for d in (2, 1, 3):
                XB.append(sems.copy(piece, G.at[t, d, oz, ys(-e)], xdev[d]))
        yield
        for s, half in ((1, pl.ds(0, X // 2)), (-1, pl.ds(X // 2, X // 2))):
            N[2 * s].wait_recv()
            piece = G.at[t, half, zh, ys(-2 * s)]
            F.append(sems.copy(piece, piece, ydev[2 * s]))
            piece = G.at[t, :, zh, ys(-2 * s)]
            F.append(sems.copy(piece, piece, ydev[s]))
        yield
        for e in (1, -1):
            N[e].wait_recv()
        for c in F + XB:
            c.wait_recv()
        parts(t)

    def width_sum(a0, na, result):
        a = pl.ds(a0, na)
        P16[a] = PF[a, oc].astype(BF16)
        cm = sems.copy(P16.at[a], C1.at[a], cdev)
        yield
        cm.wait_recv()
        zm = {}
        for d in (3, 2, 1):
            j = (zl + d) % ZL
            SZ[d, a] = (PF[a, core, j] + C1[a, j].astype(F32)).astype(BF16)
            zm[d] = sems.copy(SZ.at[d, a], RZ.at[d, a], ldev[d])
        total = PF[a, core, zl] + C1[a, zl].astype(F32)
        PF[a, core, zl] = total
        yield
        for d in (1, 3, 2):
            zm[d].wait_recv()
            total = total + RZ[d, a].astype(F32)
        PF[a, core, zl] = total
        result()

    def width_gather(a0, na):
        a = pl.ds(a0, na)
        own = H.at[a, core, zl]
        zm = {d: sems.copy(own, own, ldev[d]) for d in (3, 2, 1)}
        cm = {0: sems.copy(own, own, cdev)}
        yield
        for d in (1, 3, 2):
            zm[d].wait_recv()
            piece = H.at[a, core, (zl + ZL - d) % ZL]
            cm[d] = sems.copy(piece, piece, cdev)
        yield
        for d in (0, 1, 3, 2):
            cm[d].wait_recv()

    def make_hidden():
        g, u = PF[0, core, zl], PF[1, core, zl]
        s = 1.0 / (1.0 + jnp.exp(-g))
        H[0, core, zl] = (g * s * u).astype(BF16)

    def make_grads():
        g, u, h = PF[0, core, zl], PF[1, core, zl], PF[2, core, zl]
        s = 1.0 / (1.0 + jnp.exp(-g))
        H[1, core, zl] = (h * u * s * (1.0 + g * (1.0 - s))).astype(BF16)
        H[2, core, zl] = (h * g * s).astype(BF16)

    def scatter_a(t):
        halves = {1: pl.ds(0, X // 2), -1: pl.ds(X // 2, X // 2)}
        F4, M = {}, {}

        def send(i, v, device):
            SA[t, i] = v.astype(BF16)
            M[i] = sems.copy(SA.at[t, i], RA.at[t, i], device)

        for i, s in enumerate((1, -1)):
            SF[t, i] = OT[t, halves[s], zh, ys(4)].astype(BF16)
            F4[i] = sems.copy(SF.at[t, i], RF.at[t, i], ydev[2 * s])
            send(i, OT[t, :, zh, ys(3 * s)], ydev[s])
        for i, s in enumerate((1, -1)):
            send(2 + i, OT[t, :, zh, ys(s)], ydev[s])
        yield
        for i, s in enumerate((1, -1)):
            M[i].wait_recv()
            F4[i].wait_recv()
            OT[t, halves[s], zh, ys(2 * s)] += RF[t, i].astype(F32)
            send(4 + i, OT[t, :, zh, ys(2 * s)] + RA[t, i].astype(F32), ydev[2 * s])
        yield
        v = OT[t, :, zh, y]
        for i in (2, 3, 4, 5):
            M[i].wait_recv()
            v = v + RA[t, i].astype(F32)
        SX[t] = v[1:].astype(BF16)
        xm = {d: sems.copy(SX.at[t, d - 1], RX.at[t, d - 1], xdev[d]) for d in (2, 1, 3)}
        ACC[t] = v[0]
        yield
        for d in (1, 3, 2):
            xm[d].wait_recv()
            ACC[t] += RX[t, d - 1].astype(F32)

    def scatter_b(t):
        groups = ((0, 4), (4, 8))
        D, M = {}, []
        for lo, hi in groups:
            for n in range(lo, hi):
                SD[t, :, n] = OT[t, pl.ds(1, X - 1), oz, ys(FAR[n])].astype(BF16)
            for d in (2, 1, 3):
                at = (t, d - 1, pl.ds(lo, hi - lo))
                D[lo, d] = sems.copy(SD.at[at], RD.at[at], xdev[d])
        yield
        for lo, hi in groups:
            for d in (1, 3, 2):
                D[lo, d].wait_recv()
            for n in range(lo, hi):
                v = OT[t, 0, oz, ys(FAR[n])]
                for d in range(1, X):
                    v = v + RD[t, d - 1, n].astype(F32)
                SY[t, n] = v.astype(BF16)
                M.append(sems.copy(SY.at[t, n], RY.at[t, n], zdev[FAR[n]]))
            yield
        v = None
        for n in range(Y):
            M[n].wait_recv()
            v = RY[t, n].astype(F32) + (0.0 if v is None else v)
        SUM[t] = v

    def hid(i):
        return H[i].reshape(dw.shape[0], T)

    stores = []

    def store(src, dst):
        c = pltpu.make_async_copy(src, dst, local_sem.at[5 + len(stores)])
        c.start()
        stores.append(c)

    def grads():
        for n, (g, g_hbm) in enumerate(((gwg, gwg_hbm), (uwg, uwg_hbm))):

            @pl.loop(0, X)
            def _(d):
                g[cols((x + X - d) % X), :] = mm(block(0, d), hid(1 + n), (1, 1))

            store(g, g_hbm)
            yield

    def put(t, d, v):
        OT[t, d] = v.reshape(ZH, Y, 16, T)

    def drain(g):
        for _ in g:
            pass

    tok, cot = gather(0), gather(1)
    next(tok)
    next(cot)
    for c in loads[2:4]:
        c.wait()
    PF[...] = jnp.zeros_like(PF)

    @pl.loop(0, X)
    def _(i):
        wT[0, i] = gw[cols(i), :].T
        wT[1, i] = uw[cols(i), :].T

    loads[4].wait()
    for g in (tok, cot, tok, tok, cot, cot):
        next(g)
    drain(tok)
    pre = width_sum(0, 2, make_hidden)
    next(pre)
    next(pre)
    drain(cot)
    post = width_sum(2, 1, make_grads)
    next(post)
    next(post)

    @pl.loop(0, X)
    def _(i):
        dwT[i] = dw[:, cols(i)].T

    sems.settle()
    drain(pre)
    fore = width_gather(0, 1)
    next(fore)
    drain(post)
    back = width_gather(1, 2)
    next(back)
    drain(fore)

    @pl.loop(0, X)
    def _(d):
        put(0, d, mm(dwT[(x + d) % X], hid(0), (1, 0)))

    b0, a0, b1, a1, dw_up = scatter_b(0), scatter_a(0), scatter_b(1), scatter_a(1), grads()
    next(b0)
    next(a0)

    @pl.loop(0, X)
    def _(d):
        dwg[:, cols((x + X - d) % X)] = mm(hid(0), block(1, d), (1, 1))

    store(dwg, dwg_hbm)
    drain(back)

    @pl.loop(0, X)
    def _(d):
        i = (x + d) % X
        put(1, d, mm(gw[cols(i), :], hid(1), (1, 0)) + mm(uw[cols(i), :], hid(2), (1, 0)))

    for g in (b1, a1, b0, a0, b0, b1, a1, b1, dw_up, a0, dw_up, a1):
        next(g)
    sems.settle()
    for g in (dw_up, a0, b0, a1, b1):
        drain(g)
    for t, ref in enumerate((out_hbm, inp_hbm)):
        io[t] = (ACC[t] + SUM[t]).astype(BF16)[:, :tokens]
        store(io.at[t], ref)
    sems.settle()
    for c in stores:
        c.wait()
    assert sems.used <= send_sem.shape[0], sems.used


def hand_on(*refs):
    n = (len(refs) - 1) // 3
    src, dst, via, sem = refs[:n], refs[n : 2 * n], refs[2 * n : 3 * n], refs[-1]
    ins, outs = [], []
    for i in range(n):
        rows = src[i].shape[0]
        step = max(16, rows // PIECES)
        for at in range(0, rows, step):
            s, k = pl.ds(at, step), len(ins)
            ins.append(pltpu.make_async_copy(src[i].at[s], via[i].at[s], sem.at[0, k]))
            outs.append(pltpu.make_async_copy(via[i].at[s], dst[i].at[s], sem.at[1, k]))
    for c in ins:
        c.start()
    for i, c in enumerate(ins):
        c.wait()
        outs[i].start()
    for c in outs:
        c.wait()


def body(tokens, gate_weight, up_weight, down_weight, cotangent):
    n, (depth, hidden) = tokens.shape[0], gate_weight.shape
    T = -(-n // 128) * 128
    V = pltpu.VMEM
    part, span = hidden // (CORES * ZL), ZH * Y * 16
    scratch = [
        V((2, 16, n), BF16),
        V(gate_weight.shape, BF16), V(up_weight.shape, BF16), V(down_weight.shape, BF16),
        V((2, X, hidden, span), BF16), V((X, span, hidden), BF16),
        V(gate_weight.shape, F32), V(up_weight.shape, F32), V(down_weight.shape, F32),
        V((2, X, ZH, Y, 16, T), BF16),
        V((3, CORES, ZL, part, T), F32),
        V((3, ZL, part, T), BF16), V((3, ZL, part, T), BF16),
        V((ZL, 3, part, T), BF16), V((ZL, 3, part, T), BF16),
        V((3, CORES, ZL, part, T), BF16),
        V((2, X, ZH, Y, 16, T), F32),
        V((2, 6, X, 16, T), BF16), V((2, 6, X, 16, T), BF16),
        V((2, 2, X // 2, 16, T), BF16), V((2, 2, X // 2, 16, T), BF16),
        V((2, X - 1, 16, T), BF16), V((2, X - 1, 16, T), BF16),
        V((2, 16, T), F32),
        V((2, X - 1, Y, 16, T), BF16), V((2, X - 1, Y, 16, T), BF16),
        V((2, Y, 16, T), BF16), V((2, Y, 16, T), BF16),
        V((2, 16, T), F32),
        pltpu.SemaphoreType.DMA((200,)),
        pltpu.SemaphoreType.DMA((200,)),
        pltpu.SemaphoreType.DMA((10,)),
    ]
    anywhere = pl.BlockSpec(memory_space=pl.ANY)
    S = jax.ShapeDtypeStruct
    shapes = (
        S((16, n), BF16), S((16, n), BF16),
        S(gate_weight.shape, F32), S(up_weight.shape, F32), S(down_weight.shape, F32),
    )
    outs = pl.pallas_call(
        kernel,
        out_shape=shapes,
        in_specs=[anywhere] * 5,
        out_specs=(anywhere,) * 5,
        scratch_shapes=scratch,
        compiler_params=pltpu.CompilerParams(
            collective_id=0, has_side_effects=True, vmem_limit_bytes=60 * 2**20
        ),
        cost_estimate=pl.CostEstimate(flops=18 * n * depth * hidden, bytes_accessed=18 * depth * hidden, transcendentals=0),
        name="ffn",
    )(tokens.T, cotangent.T, gate_weight, up_weight, down_weight)
    output, input_grad, *grads = pl.pallas_call(
        hand_on,
        out_shape=shapes,
        in_specs=[anywhere] * 5,
        out_specs=(anywhere,) * 5,
        scratch_shapes=[V(a.shape, a.dtype) for a in shapes] + [pltpu.SemaphoreType.DMA((2, PIECES * len(shapes)))],
        compiler_params=pltpu.CompilerParams(vmem_limit_bytes=60 * 2**20),
        name="hand_on",
    )(*outs)
    return (output.T, input_grad.T, *grads)


def solution(mesh):
    return jax.shard_map(
        body,
        mesh=mesh,
        in_specs=(
            P(None, ("width", "blk")),
            P("width", "blk"),
            P("width", "blk"),
            P("blk", "width"),
            P(None, ("width", "blk")),
        ),
        out_specs=(
            P(None, ("width", "blk")),
            P(None, ("width", "blk")),
            P("width", "blk"),
            P("width", "blk"),
            P("blk", "width"),
        ),
        check_vma=False,
    )
```
